1024 devices in a mesh: rep: 64 (over y, x, core), ep: 16 (over z).
Axes of the slice: x: 4, y: 8, z: 16, core: 2. Of those that a mesh axis runs over, the one named last changes fastest.
Arguments:
- tokens: bfloat16 [131072, 2048], P(('rep', 'ep')), may hold values from -6 to 6
- expert_ids: int32 [131072, 1], P(('rep', 'ep')), may hold values from 0 to 15; in each aligned block of 128 rows (0 to 127, 128 to 255, ...) at most 12 rows name the same one
- gate_weights: float32 [131072, 1], P(('rep', 'ep')), may hold values from 0.2 to 1
- cotangent: bfloat16 [131072, 2048], P(('rep', 'ep')), may hold values from -6 to 6
- gate_weight: bfloat16 [16, 2048, 384], P('ep'), may hold values from -0.125 to 0.125
- up_weight: bfloat16 [16, 2048, 384], P('ep'), may hold values from -0.125 to 0.125
- down_weight: bfloat16 [16, 384, 2048], P('ep'), may hold values from -0.3125 to 0.3125
Outputs:
- layer_out: bfloat16 [131072, 2048], P(('rep', 'ep'))
- token_grad: bfloat16 [131072, 2048], P(('rep', 'ep'))
- gate_grad: float32 [131072, 1], P(('rep', 'ep'))
- down_grad: float32 [16, 384, 2048], P('ep', 'rep')
The draws below stay inside these ranges and needn't reach their ends.
Inputs may be any that keep to these rules, and one draw needn't show every extreme that they name: `expert_ids`: each token names 1 different experts. Among the rows of one device, at most 12 name the same expert, and in some devices' rows one expert is named by exactly 12.
All inputs are finite; a program needn't handle non-finite values.
Results may differ from the reference program's by a relative error of at most 0.0058.
Values may be sent and summed in bfloat16 or wider, within the bound.
A program may use at most 64 MiB of HBM per device.

```python
import math
import jax
import jax.numpy as jnp
import numpy as np
from jax import lax

D = 2048
FFW = 384
TOPK = 1
TOK_DEV = 128
EXPERTS = 16
TOKENS = 131072
CAP = 12
N_REP = 64
N_EP = 16


def block_levels(key, extent, cuts, least, high):
    gain, own = 1.0, jax.random.fold_in(key, 6)
    for dim, parts in cuts:
        steps = jnp.exp(jax.random.uniform(jax.random.fold_in(own, dim), (parts,), jnp.float32, least / len(cuts), high / len(cuts)))
        gain = gain * jnp.repeat(steps, extent[dim] // parts).reshape([-1 if axis == dim else 1 for axis in range(len(extent))])
    return gain


def shared_out(rng, own, number, rows, count, top, bound, skew):
    sequence = jax.random.permutation(rng, count)
    heavy_load, usual = load_shares(count, rows * top, bound, skew, True), load_shares(count, rows * top, bound, skew, False)
    places = jnp.arange(count)

    def named(lengths, rotation):
        used = int((lengths > 0).sum())
        fixed = max(1, used // 4)
        moved = fixed + (places - fixed + rotation * (used - fixed)) % max(1, count - fixed)
        return jnp.zeros((count,), jnp.int32).at[sequence[jnp.where(places < fixed, places, moved)]].set(jnp.asarray(lengths, jnp.int32))

    lengths = jnp.where(number % 4 == 0, named(heavy_load, number // 4), named(usual, number - number // 4 - 1))
    mixed = jax.random.permutation(jax.random.fold_in(own, 3), count)
    donor, taker = mixed[0:count // 2 * 2:2], mixed[1:count // 2 * 2:2]
    room = jnp.minimum(lengths[donor] - 1, bound - lengths[taker]) // 2
    room = jnp.where((donor == sequence[0]) | (taker == sequence[0]) | (lengths[taker] == 0), 0, jnp.maximum(room, 0))
    moved = jax.random.randint(jax.random.fold_in(own, 4), (count // 2,), 0, 1 << 20) % (room + 1)
    lengths = lengths.at[donor].add(-moved).at[taker].add(moved)
    labels = jnp.searchsorted(jnp.cumsum(lengths), jnp.arange(rows * top), side="right").astype(jnp.int32)
    grid = labels.reshape(top, rows).T
    grid = grid[jax.random.permutation(jax.random.fold_in(own, 1), rows)]
    rotation = jax.random.randint(jax.random.fold_in(own, 2), (rows, 1), 0, top)
    return jnp.take_along_axis(grid, (jnp.arange(top)[None, :] + rotation) % top, axis=1)


def load_shares(number_of, total, bound, lean, full):
    portions = [(1 << 20) // math.isqrt(rank ** lean) + 1 for rank in range(1, number_of + 1)]
    largest = bound if full else min(bound, max(-(-total // number_of), total * portions[0] // sum(portions)))
    least = 1 if total - largest >= number_of - 1 else 0
    given, rest = [largest] + [least] * (number_of - 1), total - largest - least * (number_of - 1)
    while rest > 0:
        free = [i for i in range(1, number_of) if given[i] < largest] or [i for i in range(1, number_of) if given[i] < bound]
        mass, left = sum([portions[i] for i in free]), rest
        for i in free:
            extra = min(bound - given[i], max(1, left * portions[i] // mass), rest)
            given[i] = given[i] + extra
            rest = rest - extra
    return np.array(given)


def scatter_about(rng, shape, width, limit, pieces=(), kind=jnp.bfloat16):
    result = jax.random.normal(rng, shape, jnp.float32) * width
    if len(pieces) > 0:
        result = block_levels(rng, shape, pieces, -0.22, 0.18) * result
    return jnp.clip(result, min=-limit, max=limit).astype(kind)


def setup_inputs(seed: int = 0) -> dict:
    key_of = jax.random.split(jax.random.key(seed), 8)
    tokens = scatter_about(key_of[0], (TOKENS, D), 1.0, 6.0, ((0, 1024),))
    expert_ids_keys = jax.random.split(jax.random.fold_in(key_of[1], 1), TOKENS // TOK_DEV)
    expert_ids_turns = jax.random.permutation(jax.random.fold_in(key_of[1], 3), TOKENS // TOK_DEV)
    expert_ids = jax.vmap(lambda own, number: shared_out(jax.random.fold_in(key_of[1], 2), own, number, TOK_DEV, EXPERTS, TOPK, CAP, 2))(expert_ids_keys, expert_ids_turns).reshape((TOKENS, TOPK))
    gate_weights = jnp.clip(0.2 + 0.8 * jax.random.uniform(key_of[2], (TOKENS, TOPK), jnp.float32) ** block_levels(key_of[2], (TOKENS, TOPK), ((0, 1024),), -0.2, 0.2), 0.2, 1.0)
    cotangent = scatter_about(key_of[3], (TOKENS, D), 1.0, 6.0, ((0, 1024),))
    gate_weight = scatter_about(key_of[4], (EXPERTS, D, FFW), D ** -0.5, 0.125, ((0, 16),))
    up_weight = scatter_about(key_of[5], (EXPERTS, D, FFW), D ** -0.5, 0.125, ((0, 16),))
    down_weight = scatter_about(key_of[6], (EXPERTS, FFW, D), FFW ** -0.5, 0.3125, ((0, 16),))
    return dict(tokens=tokens, expert_ids=expert_ids, gate_weights=gate_weights, cotangent=cotangent, gate_weight=gate_weight, up_weight=up_weight, down_weight=down_weight)


def reference(tokens, expert_ids, gate_weights, cotangent, gate_weight, up_weight, down_weight):
    rows_all = TOKENS * TOPK
    span = N_REP * N_EP * CAP
    flat_ids = expert_ids.reshape(rows_all).astype(jnp.int32)
    order = jnp.argsort(flat_ids, stable=True).astype(jnp.int32)
    inverse = jnp.argsort(order, stable=True).astype(jnp.int32)
    counts = jnp.sum((flat_ids[:, None] == jnp.arange(EXPERTS, dtype=jnp.int32)[None, :]).astype(jnp.int32), axis=0)
    starts = (jnp.cumsum(counts) - counts).astype(jnp.int32)
    token_of = (order // TOPK).astype(jnp.int32)
    gate_rows = gate_weights.reshape(rows_all, 1)
    cot_rows = jnp.repeat(cotangent, TOPK, axis=0)
    dout_rows = (gate_rows * cot_rows.astype(jnp.float32)).astype(jnp.bfloat16)
    x_sorted = jnp.concatenate([tokens[token_of], jnp.zeros((span, D), tokens.dtype)], axis=0)
    d_sorted = jnp.concatenate([dout_rows[order], jnp.zeros((span, D), dout_rows.dtype)], axis=0)
    out_buf = jnp.zeros((rows_all + span, D), jnp.bfloat16)
    back_buf = jnp.zeros((rows_all + span, D), jnp.bfloat16)

    def per_expert(carry, expert):
        out_buf, back_buf = carry
        start = starts[expert].astype(jnp.int32)
        inside = (jnp.arange(span, dtype=jnp.int32) < counts[expert])[:, None]
        row_x = jnp.where(inside, lax.dynamic_slice_in_dim(x_sorted, start, span, 0), jnp.zeros((), x_sorted.dtype))
        row_d = jnp.where(inside, lax.dynamic_slice_in_dim(d_sorted, start, span, 0), jnp.zeros((), d_sorted.dtype))
        w_gate_one = gate_weight[expert]
        w_up_one = up_weight[expert]
        w_down_one = down_weight[expert]
        gate_pre = jnp.dot(row_x, w_gate_one, preferred_element_type=jnp.float32)
        up_pre = jnp.dot(row_x, w_up_one, preferred_element_type=jnp.float32)
        gate_act = jax.nn.silu(gate_pre)
        hidden = (gate_act * up_pre).astype(jnp.bfloat16)
        expert_out = jnp.dot(hidden, w_down_one, preferred_element_type=jnp.float32).astype(jnp.bfloat16)
        hidden_grad = jnp.dot(row_d, w_down_one.T, preferred_element_type=jnp.float32)
        sigma = jax.nn.sigmoid(gate_pre)
        gate_back = (hidden_grad * up_pre * sigma * (1.0 + gate_pre * (1.0 - sigma))).astype(jnp.bfloat16)
        up_back = (hidden_grad * gate_act).astype(jnp.bfloat16)
        input_back = (jnp.dot(gate_back, w_gate_one.T, preferred_element_type=jnp.float32)
                      + jnp.dot(up_back, w_up_one.T, preferred_element_type=jnp.float32)).astype(jnp.bfloat16)
        weight_grad = jnp.dot(hidden.T, row_d, preferred_element_type=jnp.float32)
        old_out = lax.dynamic_slice_in_dim(out_buf, start, span, 0)
        old_back = lax.dynamic_slice_in_dim(back_buf, start, span, 0)
        out_buf = lax.dynamic_update_slice_in_dim(out_buf, jnp.where(inside, expert_out, old_out), start, 0)
        back_buf = lax.dynamic_update_slice_in_dim(back_buf, jnp.where(inside, input_back, old_back), start, 0)
        return (out_buf, back_buf), weight_grad

    (out_buf, back_buf), down_grad = lax.scan(per_expert, (out_buf, back_buf), jnp.arange(EXPERTS, dtype=jnp.int32))
    out_rows = out_buf[:rows_all][inverse].astype(jnp.float32)
    back_rows = back_buf[:rows_all][inverse].astype(jnp.float32)
    layer_out = jnp.sum((gate_rows * out_rows).reshape(TOKENS, TOPK, D), axis=1).astype(jnp.bfloat16)
    gate_grad = jnp.sum(cot_rows.astype(jnp.float32) * out_rows, axis=1).reshape(TOKENS, TOPK)
    token_grad = jnp.sum(back_rows.reshape(TOKENS, TOPK, D), axis=1).astype(jnp.bfloat16)
    return (layer_out, token_grad, gate_grad, down_grad)
```

```python
import jax
import jax.numpy as jnp
import numpy as np
from jax import lax
from jax.experimental import pallas as pl
from jax.experimental.pallas import tpu as pltpu
from jax.sharding import PartitionSpec as P

NX, NY, NZ = 4, 8, 16
TOK, WIDTH, FFW = 128, 2048, 384
CAP = 12
HALF = WIDTH // 2
BLK = 4 * CAP
ROWS = NZ * BLK
SLOTS = NZ * CAP
GROWS = WIDTH // (NX * NY)
DROWS = FFW // NY
QCOL = WIDTH // NX
MESH = pl.DeviceIdType.MESH
F32 = jnp.float32
BF16 = jnp.bfloat16
NT = (((1,), (1,)), ((), ()))


def dot(a, b):
    return jnp.dot(a, b, preferred_element_type=F32)


def dot_nt(a, b):
    return lax.dot_general(a, b, NT, preferred_element_type=F32)


def kernel(
    x_hbm, cot_hbm, ids_row, ids_col, gw_ref, wg_hbm, wu_hbm, wd_hbm, perm_hbm, wantc,
    out_ref, tgrad_ref, ggrad_ref, dgrad_ref,
    x, cot, z, wg, wu, wd, perm, send, recv, xall, yall, rsend, rrecv,
    dw, dwb, xrecv, ysend, yb, yrecv, zsend, zrecv, fsend, frecv,
    loc_sem, s1, r1, s2, r2, wzs, wzr, wxs, wxr, wys, wyr,
    dxs, dxr, dys, dyr, dzs, dzr, fs, fr,
):
    rep = lax.axis_index("rep")
    pz = lax.axis_index("ep")
    core = lax.rem(rep, 2)
    px = lax.rem(rep // 2, NX)
    py = rep // (2 * NX)
    other = 1 - core

    def dev(y, x_, c, z_):
        return ((y * NX + x_) * 2 + c, z_)

    def mod(v, n):
        return lax.rem(v + n, n)

    def at_z(off, c):
        return dev(py, px, c, mod(pz + off, NZ))

    tie = 4 - 8 * core

    def remote(src, dst, ss, rs, target):
        return pltpu.make_async_remote_copy(
            src_ref=src, dst_ref=dst, send_sem=ss, recv_sem=rs,
            device_id=target, device_id_type=MESH,
        )

    barrier = pltpu.get_barrier_semaphore()
    peers = [at_z(o, core) for o in (-4, -3, -2, -1, 1, 2, 3, 4, 8)]
    peers += [at_z(o, other) for o in (-3, -2, -1, 0, 1, 2, 3, 8)] + [at_z(tie, other)]
    for k in range(1, NX):
        peers.append(dev(py, mod(px + k, NX), core, pz))
        peers.append(dev(py, mod(px + k, NX), other, pz))
    for k in range(1, NY):
        peers.append(dev(mod(py + k, NY), px, core, pz))
    for peer in peers:
        pl.semaphore_signal(barrier, inc=1, device_id=peer, device_id_type=MESH)

    loads = [
        pltpu.make_async_copy(x_hbm, x, loc_sem.at[0]),
        pltpu.make_async_copy(cot_hbm, cot, loc_sem.at[1]),
        pltpu.make_async_copy(perm_hbm, perm, loc_sem.at[2]),
    ]
    for c in loads:
        c.start()
    wloads = [
        pltpu.make_async_copy(wg_hbm, wg, loc_sem.at[3]),
        pltpu.make_async_copy(wu_hbm, wu, loc_sem.at[4]),
        pltpu.make_async_copy(wd_hbm, wd, loc_sem.at[5]),
    ]

    @pl.when(core == 0)
    def _():
        for c in wloads:
            c.start()

    relr = lax.rem(ids_row[...] - pz + NZ, NZ)
    oh_r = (lax.broadcasted_iota(jnp.int32, (NZ, TOK), 0) == relr).astype(F32)
    up_tri = (
        lax.broadcasted_iota(jnp.int32, (TOK, TOK), 0)
        < lax.broadcasted_iota(jnp.int32, (TOK, TOK), 1)
    ).astype(F32)
    before = dot(oh_r.astype(BF16), up_tri.astype(BF16))
    slot_r = jnp.sum(before * oh_r, axis=0, keepdims=True).astype(jnp.int32)
    tgt_r = relr * CAP + slot_r

    ex = lax.broadcasted_iota(jnp.int32, (NZ, BLK, TOK), 0)
    row = lax.broadcasted_iota(jnp.int32, (NZ, BLK, TOK), 1)
    half = jnp.where(row >= 2 * CAP, 1, 0)
    row = row - 2 * CAP * half
    kind = jnp.where(row >= CAP, 1, 0)
    want = ex * CAP + row - CAP * kind
    quarter = jnp.where(want == tgt_r.reshape(1, 1, TOK), kind * 2 + half, -1)
    place = jnp.concatenate(
        [
            jnp.where(quarter == b, 1.0, 0.0).reshape(ROWS, TOK).astype(BF16)
            for b in range(4)
        ],
        axis=1,
    )
    for c in loads:
        c.wait()
    z[0:TOK, :] = x[:, :HALF]
    z[TOK : 2 * TOK, :] = x[:, HALF:]
    dout = (gw_ref[...] * cot[...].astype(F32)).astype(BF16)
    z[2 * TOK : 3 * TOK, :] = dout[:, :HALF]
    z[3 * TOK :, :] = dout[:, HALF:]

    @pl.loop(0, 4)
    def _(n):
        cols = pl.ds(pl.multiple_of(n * 256, 256), 256)
        send[:, :, cols] = dot(place, z[:, cols]).astype(BF16).reshape(NZ, BLK, 256)

    pl.semaphore_wait(barrier, len(peers))

    row_g = pl.multiple_of(py * (NX * GROWS) + px * GROWS, GROWS)
    row_d = pl.multiple_of(py * DROWS, 16)
    col_d = pl.multiple_of(px * QCOL, QCOL)

    def slices(y, x_, whole):
        if whole:
            g = pl.ds(pl.multiple_of(y * (NX * GROWS), NX * GROWS), NX * GROWS)
            return [(g, slice(None)), (g, slice(None)),
                    (pl.ds(pl.multiple_of(y * DROWS, 16), DROWS), slice(None))]
        g = pl.ds(pl.multiple_of(y * (NX * GROWS) + x_ * GROWS, GROWS), GROWS)
        d = (pl.ds(pl.multiple_of(y * DROWS, 16), DROWS),
             pl.ds(pl.multiple_of(x_ * QCOL, QCOL), QCOL))
        return [(g, slice(None)), (g, slice(None)), d]

    weights = (wg, wu, wd)
    own = slices(py, px, False)
    wz = [
        remote(h.at[i], w.at[i], wzs.at[m], wzr.at[m], at_z(8, core))
        for m, (h, w, i) in enumerate(zip((wg_hbm, wu_hbm, wd_hbm), weights, own))
    ]

    @pl.when(core == 1)
    def _():
        for c in wz:
            c.start()

    def out_copy(off, dc):
        d = mod(off + 8 * dc, NZ)
        k = core * 8 + off + 3 + core
        return remote(send.at[d], recv.at[k], s1.at[d], r1.at[k], at_z(off, dc))

    def back_copy(off, cs):
        k = cs * 8 + off + 3 + cs
        d = mod(off + 8 * core, NZ)
        return remote(rsend.at[k], rrecv.at[d], s2.at[k], r2.at[d], at_z(-off, cs))

    order = [(tie, core), (tie, other)]
    for o in (3, 2, 1):
        order += [(o, core), (-o, core), (o, other), (-o, other)]
    order += [(0, other)]
    outs = [out_copy(off, dc) for off, dc in order]
    for c in outs:
        c.start()
    mine_d = 8 * core
    mine_k = core * 8 + 3 + core
    self_out = pltpu.make_async_copy(send.at[mine_d], recv.at[mine_k], loc_sem.at[6])
    self_out.start()

    @pl.when(core == 1)
    def _():
        for c in wz:
            c.wait_recv()
        xs = []
        for k in (2, 1, 3):
            to = dev(py, mod(px + k, NX), core, pz)
            for m in range(3):
                xs.append(
                    remote(weights[m].at[own[m]], weights[m].at[own[m]],
                           wxs.at[k - 1, m], wxr.at[k - 1, m], to)
                )
        for c in xs:
            c.start()
        for k in (1, 3, 2):
            src = slices(py, mod(px - k, NX), False)
            for m in range(3):
                w = weights[m].at[src[m]]
                remote(w, w, wxs.at[k - 1, m], wxr.at[k - 1, m],
                       dev(py, mod(px + k, NX), core, pz)).wait_recv()
        ys = []
        depth = ((4, 3), (3, 4), (4, 3))
        for step in range(5):
            for m in range(3):
                for side, sign in ((0, 1), (1, -1)):
                    if step > depth[m][side]:
                        continue
                    w = weights[m].at[slices(mod(py - sign * step, NY), px, True)[m]]
                    to = dev(mod(py + sign, NY), px, core, pz)
                    if step > 0:
                        remote(w, w, wys.at[side, m, step - 1], wyr.at[side, m, step - 1],
                               to).wait_recv()
                    if step < depth[m][side]:
                        c = remote(w, w, wys.at[side, m, step], wyr.at[side, m, step], to)
                        c.start()
                        ys.append(c)
        for c in wz + xs + ys:
            c.wait_send()

    @pl.when(core == 0)
    def _():
        for c in wloads:
            c.wait()

    self_out.wait()

    def in_copy(off, cs):
        k = cs * 8 + off + 3 + cs
        d = mod(off + 8 * core, NZ)
        return remote(send.at[d], recv.at[k], s1.at[d], r1.at[k], at_z(-off, cs))

    sources = [(tie, core), (4 - 8 * other, other)]
    for o in (3, 2, 1):
        sources += [(o, core), (-o, core), (o, other), (-o, other)]
    sources += [(0, other)]
    for off, cs in sources:
        in_copy(off, cs).wait_recv()

    @pl.loop(0, 4)
    def _(n):
        cols = pl.ds(pl.multiple_of(n * 256, 256), 256)
        xall[:, cols] = dot(perm[0], recv[:, :, cols].reshape(ROWS, 256)).astype(BF16)

    xl, xr = xall[0:SLOTS, :], xall[SLOTS : 2 * SLOTS, :]
    dl, dr = xall[2 * SLOTS : 3 * SLOTS, :], xall[3 * SLOTS :, :]
    a = dot(xl, wg[:HALF, :]) + dot(xr, wg[HALF:, :])
    b = dot(xl, wu[:HALF, :]) + dot(xr, wu[HALF:, :])
    dh = dot_nt(dl, wd[:, :HALF]) + dot_nt(dr, wd[:, HALF:])
    s = 1.0 / (1.0 + jnp.exp(-a))
    act = a * s
    hf = act * b
    h = hf.astype(BF16)
    da = (dh * b * s * (1.0 + a * (1.0 - s))).astype(BF16)
    db = (dh * act).astype(BF16)
    ht = jnp.transpose(hf).astype(BF16)
    for j in range(NX):
        d0 = 2 * SLOTS + SLOTS * (j // 2)
        c0 = QCOL * (j % 2)
        piece = dot(ht, xall[d0 : d0 + SLOTS, c0 : c0 + QCOL])
        dw[j] = piece
        dwb[j] = piece.astype(BF16)
    dx_copies = []
    for k in (2, 1, 3):
        to = mod(px + k, NX)
        c = remote(dwb.at[to], xrecv.at[k - 1], dxs.at[k - 1], dxr.at[k - 1],
                   dev(py, to, core, pz))
        c.start()
        dx_copies.append(c)

    for n in range(4):
        q, c0 = n // 2, QCOL * (n % 2)
        cols = slice(n * QCOL, (n + 1) * QCOL)
        yall[q * SLOTS : (q + 1) * SLOTS, c0 : c0 + QCOL] = dot(h, wd[:, cols]).astype(BF16)
        back = dot_nt(da, wg[cols, :]) + dot_nt(db, wu[cols, :])
        yall[(2 + q) * SLOTS : (3 + q) * SLOTS, c0 : c0 + QCOL] = back.astype(BF16)

    @pl.loop(0, 4)
    def _(n):
        cols = pl.ds(pl.multiple_of(n * 256, 256), 256)
        rsend[:, :, cols] = dot(perm[1], yall[:, cols]).astype(BF16).reshape(NZ, BLK, 256)

    backs = [back_copy(off, cs) for off, cs in sources]
    for c in backs:
        c.start()
    self_back = pltpu.make_async_copy(rsend.at[mine_k], rrecv.at[mine_d], loc_sem.at[7])
    self_back.start()

    for c in dx_copies:
        c.wait_recv()
    for i in range(NY):
        rr = slice(i * DROWS, (i + 1) * DROWS)
        part = dw[px, rr, :]
        for k in range(NX - 1):
            part = part + xrecv[k, rr, :].astype(F32)
        ysend[i] = part
        yb[i] = part.astype(BF16)
    dy_copies = []
    for k in (4, 3, 5, 2, 6, 1, 7):
        to = mod(py + k, NY)
        c = remote(yb.at[to], yrecv.at[k - 1], dys.at[k - 1], dyr.at[k - 1],
                   dev(to, px, core, pz))
        c.start()
        dy_copies.append(c)
    for c in dy_copies:
        c.wait_recv()
    part = ysend[py]
    for k in range(NY - 1):
        part = part + yrecv[k].astype(F32)
    zsend[...] = part
    dz = remote(zsend, zrecv, dzs.at[0], dzr.at[0], at_z(8, other))

    @pl.when(core == 1)
    def _():
        dz.start()

    @pl.when(core == 0)
    def _():
        dz.wait_recv()
        total = zsend[...] + zrecv[...]
        for i in range(2 * NX):
            fsend[i, 0:6, :] = total[i * 6 : (i + 1) * 6, :]
            fsend[i, 6:8, :] = jnp.zeros((2, QCOL), F32)
        mine = pltpu.make_async_copy(fsend.at[2 * px], frecv.at[px], loc_sem.at[8])
        mine.start()
        fins = [remote(fsend.at[2 * px + 1], frecv.at[px], fs.at[0, 1], fr.at[px],
                       dev(py, px, 1, pz))]
        for k in range(1, NX):
            to = mod(px + k, NX)
            for c in range(2):
                fins.append(
                    remote(fsend.at[2 * to + c], frecv.at[px], fs.at[k, c], fr.at[px],
                           dev(py, to, c, pz))
                )
        for c in fins:
            c.start()
        mine.wait()
        for k in range(1, NX):
            src = mod(px + k, NX)
            remote(fsend.at[0], frecv.at[src], fs.at[k, 0], fr.at[src],
                   dev(py, src, 0, pz)).wait_recv()
        for c in fins:
            c.wait_send()

    @pl.when(core == 1)
    def _():
        for src in range(NX):
            remote(fsend.at[0], frecv.at[src], fs.at[0, 0], fr.at[src],
                   dev(py, src, 0, pz)).wait_recv()
        dz.wait_send()

    for j in range(NX):
        dgrad_ref[0, :, j * QCOL : (j + 1) * QCOL] = frecv[j, 0:6, :]

    relc = lax.rem(ids_col[...] - pz + NZ, NZ)
    oh_c = (lax.broadcasted_iota(jnp.int32, (TOK, TOK), 1) == relc).astype(F32)
    lo_tri = (
        lax.broadcasted_iota(jnp.int32, (TOK, TOK), 0)
        > lax.broadcasted_iota(jnp.int32, (TOK, TOK), 1)
    ).astype(F32)
    before_c = dot(lo_tri.astype(BF16), oh_c.astype(BF16))
    slot_c = jnp.sum(before_c * oh_c, axis=1, keepdims=True).astype(jnp.int32)
    tgt_c = relc * CAP + slot_c
    takes = [
        jnp.where(wantc[b : b + 1, :] == tgt_c, 1.0, 0.0).astype(BF16) for b in range(4)
    ]
    self_back.wait()

    def ret_copy(off, dc):
        d = mod(off + 8 * dc, NZ)
        k = core * 8 + off + 3 + core
        return remote(rsend.at[k], rrecv.at[d], s2.at[k], r2.at[d], at_z(off, dc))

    for off, dc in order:
        ret_copy(off, dc).wait_recv()
    gsum = jnp.zeros((TOK, 1), F32)
    for n in range(4):
        cols = slice(n * 256, (n + 1) * 256)
        src = rrecv[:, :, cols].reshape(ROWS, 256)
        for q in range(2):
            full = slice(q * HALF + n * 256, q * HALF + (n + 1) * 256)
            o = dot(takes[q], src)
            out_ref[:, full] = (gw_ref[...] * o).astype(BF16)
            gsum = gsum + jnp.sum(cot[:, full].astype(F32) * o, axis=1, keepdims=True)
            tgrad_ref[:, full] = dot(takes[2 + q], src).astype(BF16)
    ggrad_ref[...] = gsum

    for c in outs + backs + dx_copies + dy_copies:
        c.wait_send()


def tables():
    perm = np.zeros((ROWS, ROWS), np.float32)
    want = np.full((8, ROWS), -1, np.int32)
    for r in range(ROWS):
        k, w = divmod(r, BLK)
        half, w = divmod(w, 2 * CAP)
        kind, s = divmod(w, CAP)
        b = kind * 2 + half
        perm[b * SLOTS + k * CAP + s, r] = 1.0
        want[b, r] = k * CAP + s
    return np.stack([perm, perm.T]), want


def shards(tokens, expert_ids, gate_weights, cotangent, gate_weight, up_weight, down_weight):
    perm, want = tables()
    hbm = pl.BlockSpec(memory_space=pl.ANY)
    vmem = pl.BlockSpec(memory_space=pltpu.VMEM)
    dma = pltpu.SemaphoreType.DMA
    return pl.pallas_call(
        kernel,
        out_shape=(
            jax.ShapeDtypeStruct((TOK, WIDTH), BF16),
            jax.ShapeDtypeStruct((TOK, WIDTH), BF16),
            jax.ShapeDtypeStruct((TOK, 1), F32),
            jax.ShapeDtypeStruct((1, FFW // (2 * NX * NY), WIDTH), F32),
        ),
        in_specs=[hbm, hbm, vmem, vmem, vmem, hbm, hbm, hbm, hbm, vmem],
        out_specs=(vmem, vmem, vmem, vmem),
        scratch_shapes=[
            pltpu.VMEM((TOK, WIDTH), BF16),
            pltpu.VMEM((TOK, WIDTH), BF16),
            pltpu.VMEM((4 * TOK, HALF), BF16),
            pltpu.VMEM((WIDTH, FFW), BF16),
            pltpu.VMEM((WIDTH, FFW), BF16),
            pltpu.VMEM((FFW, WIDTH), BF16),
            pltpu.VMEM((2, ROWS, ROWS), BF16),
            pltpu.VMEM((NZ, BLK, HALF), BF16),
            pltpu.VMEM((NZ, BLK, HALF), BF16),
            pltpu.VMEM((ROWS, HALF), BF16),
            pltpu.VMEM((ROWS, HALF), BF16),
            pltpu.VMEM((NZ, BLK, HALF), BF16),
            pltpu.VMEM((NZ, BLK, HALF), BF16),
            pltpu.VMEM((NX, FFW, QCOL), F32),
            pltpu.VMEM((NX, FFW, QCOL), BF16),
            pltpu.VMEM((NX - 1, FFW, QCOL), BF16),
            pltpu.VMEM((NY, DROWS, QCOL), F32),
            pltpu.VMEM((NY, DROWS, QCOL), BF16),
            pltpu.VMEM((NY - 1, DROWS, QCOL), BF16),
            pltpu.VMEM((DROWS, QCOL), F32),
            pltpu.VMEM((DROWS, QCOL), F32),
            pltpu.VMEM((2 * NX, 8, QCOL), F32),
            pltpu.VMEM((NX, 8, QCOL), F32),
            dma((9,)),
            dma((NZ,)), dma((NZ,)), dma((NZ,)), dma((NZ,)),
            dma((3,)), dma((3,)), dma((3, 3)), dma((3, 3)),
            dma((2, 3, 4)), dma((2, 3, 4)),
            dma((NX - 1,)), dma((NX - 1,)), dma((NY - 1,)), dma((NY - 1,)),
            dma((1,)), dma((1,)), dma((NX, 2)), dma((NX,)),
        ],
        compiler_params=pltpu.CompilerParams(
            collective_id=0, has_side_effects=True, vmem_limit_bytes=56 * 1024 * 1024
        ),
        cost_estimate=pl.CostEstimate(
            flops=6_000_000_000, bytes_accessed=16_000_000, transcendentals=100_000
        ),
    )(
        tokens, cotangent, expert_ids.reshape(1, TOK), expert_ids, gate_weights,
        gate_weight[0], up_weight[0], down_weight[0],
        jnp.asarray(perm, BF16), jnp.asarray(want),
    )


def solution(mesh):
    rows = P(("rep", "ep"), None)
    weight = P("ep", None, None)
    return jax.shard_map(
        shards,
        mesh=mesh,
        in_specs=(rows, rows, rows, rows, weight, weight, weight),
        out_specs=(rows, rows, rows, P("ep", "rep", None)),
        check_vma=False,
    )
```

```python
import jax
import jax.numpy as jnp
import numpy as np
from jax import lax
from jax.experimental import pallas as pl
from jax.experimental.pallas import tpu as pltpu
from jax.sharding import PartitionSpec as P

NX, NY, NZ = 4, 8, 16
TOK, WIDTH, FFW = 128, 2048, 384
CAP = 12
HALF = WIDTH // 2
BLK = 4 * CAP
FAR = 6
NEAR = NZ - FAR
FROWS, NROWS = FAR * BLK, NEAR * BLK
FPAD, NPAD = 80, 128
GROWS = WIDTH // (NX * NY)
DROWS = FFW // NY
QCOL = WIDTH // NX
MID = FFW // 2
MESH = pl.DeviceIdType.MESH
F32 = jnp.float32
BF16 = jnp.bfloat16
NT = (((1,), (1,)), ((), ()))
ALL = slice(None)


def dot(a, b):
    return jnp.dot(a, b, preferred_element_type=F32)


def dot_nt(a, b):
    return lax.dot_general(a, b, NT, preferred_element_type=F32)


def ds(start, size):
    return pl.ds(pl.multiple_of(start, size), size)


def kernel(
    x_hbm, cot_hbm, ids_row, gw_row, wg_hbm, wu_hbm, wd_hbm, pf_hbm, pft_hbm, pn_hbm, pnt_hbm,
    wantc,
    out_ref, tgrad_ref, ggrad_ref, dgrad_ref,
    x, cot, z, wg, wu, wd, pf, pft, pn, pnt, send, recv, xf, yf, xn, yn, rsend, rrecv,
    oacc, dw, dwb, opp, pure, msend, mrecv, ysum, yb, yrecv, zsend, zrecv, fsend, frecv,
    loc_sem, s1, r1, s2, r2, wzs, wzr, gxs, gxr, gys, gyr, uys, uyr, uxs, uxr,
    dxs, dxr, dys, dyr, dzs, dzr, fs, fr,
):
    rep = lax.axis_index("rep")
    pz = lax.axis_index("ep")
    core = lax.rem(rep, 2)
    px = lax.rem(rep // 2, NX)
    py = rep // (2 * NX)
    other = 1 - core

    def dev(y, x_, c, z_):
        return ((y * NX + x_) * 2 + c, z_)

    def mod(v, n):
        return lax.rem(v + n, n)

    def at_x(k):
        return dev(py, mod(px + k, NX), core, pz)

    def at_y(k):
        return dev(mod(py + k, NY), px, core, pz)

    def at_z(off, c):
        return dev(py, px, c, mod(pz + off, NZ))

    def remote(src, dst, ss, rs, target):
        return pltpu.make_async_remote_copy(
            src_ref=src, dst_ref=dst, send_sem=ss, recv_sem=rs,
            device_id=target, device_id_type=MESH,
        )

    tie, tie_other = 4 - 8 * core, 4 - 8 * other
    barrier = pltpu.get_barrier_semaphore()
    peers = [at_z(o, core) for o in (-4, -3, -2, -1, 1, 2, 3, 4, 8)]
    peers += [at_z(o, other) for o in (-3, -2, -1, 0, 1, 2, 3, 8)] + [at_z(tie, other)]
    for k in range(1, NX):
        peers.append(at_x(k))
        peers.append(dev(py, mod(px + k, NX), other, pz))
    for k in range(1, NY):
        peers.append(at_y(k))
    for peer in peers:
        pl.semaphore_signal(barrier, inc=1, device_id=peer, device_id_type=MESH)

    loads = [
        pltpu.make_async_copy(s, d, loc_sem.at[i])
        for i, (s, d) in enumerate(
            ((x_hbm, x), (cot_hbm, cot), (pf_hbm, pf), (pft_hbm, pft), (pn_hbm, pn), (pnt_hbm, pnt))
        )
    ]
    for c in loads:
        c.start()
    weights = (wg, wu, wd)
    wloads = [
        pltpu.make_async_copy(s, d, loc_sem.at[6 + i])
        for i, (s, d) in enumerate(zip((wg_hbm, wu_hbm, wd_hbm), weights))
    ]

    @pl.when(core == 0)
    def _():
        for c in wloads:
            c.start()

    def place_of(ids):
        u = lax.rem(ids - pz + (2 * NZ - 3), NZ)
        u = u + jnp.where((u >= 3) & (u < 8), 3, 0) - jnp.where((u >= 8) & (u < 11), 5, 0)
        return u

    lane = lax.broadcasted_iota(jnp.int32, (TOK, TOK), 1)
    sub = lax.broadcasted_iota(jnp.int32, (TOK, TOK), 0)
    eye = lane == sub
    q_r = place_of(ids_row[...])
    q_c = jnp.sum(jnp.where(eye, q_r, 0), axis=1, keepdims=True)
    gw_c = jnp.sum(jnp.where(eye, gw_row[...], 0.0), axis=1, keepdims=True)
    oh_r = (lax.broadcasted_iota(jnp.int32, (NZ, TOK), 0) == q_r).astype(F32)
    before = dot(oh_r.astype(BF16), (sub < lane).astype(F32).astype(BF16))
    slot_r = jnp.sum(before * oh_r, axis=0, keepdims=True).astype(jnp.int32)
    tgt_r = q_r * CAP + slot_r
    tgt_c = jnp.sum(jnp.where(eye, tgt_r, 0), axis=1, keepdims=True)

    def placing(first, count):
        ex = lax.broadcasted_iota(jnp.int32, (count, BLK, TOK), 0) + first
        row = lax.broadcasted_iota(jnp.int32, (count, BLK, TOK), 1)
        half = jnp.where(row >= 2 * CAP, 1, 0)
        row = row - 2 * CAP * half
        kind = jnp.where(row >= CAP, 1, 0)
        want = ex * CAP + row - CAP * kind
        quarter = jnp.where(want == tgt_r.reshape(1, 1, TOK), kind * 2 + half, -1)
        return jnp.concatenate(
            [
                jnp.where(quarter == b, 1.0, 0.0).reshape(count * BLK, TOK).astype(BF16)
                for b in range(4)
            ],
            axis=1,
        )

    for c in loads:
        c.wait()
    z[0:TOK, :] = x[:, :HALF]
    z[TOK : 2 * TOK, :] = x[:, HALF:]
    dout = (gw_c * cot[...].astype(F32)).astype(BF16)
    z[2 * TOK : 3 * TOK, :] = dout[:, :HALF]
    z[3 * TOK :, :] = dout[:, HALF:]

    pl.semaphore_wait(barrier, len(peers))

    own = (
        (ds(py * (NX * GROWS) + px * GROWS, GROWS), ALL),
        (ds(px * (NY * GROWS) + py * GROWS, GROWS), ALL),
        (ds(py * DROWS, DROWS), ds(px * QCOL, QCOL)),
    )
    wz = [
        remote(h.at[i], w.at[i], wzs.at[m], wzr.at[m], at_z(8, core))
        for m, (h, w, i) in enumerate(zip((wg_hbm, wu_hbm, wd_hbm), weights, own))
    ]

    @pl.when(core == 1)
    def _():
        for m in (1, 2, 0):
            wz[m].start()

    def as_source():
        far = [(tie, core, 1, 4 + core), (tie, other, 4, 4 + core)]
        for c in (core, other):
            far += [(3, c, 3 * c, 2 + core), (-3, c, 5 - 3 * c, core)]
        near = []
        for o in (2, -2, 1, -1):
            for c in (core, other):
                near.append((o, c, 13 + o - 5 * c, 10 + 2 * o + core))
        near.append((0, other, 13 - 5 * other, 10 + core))
        return far, near

    def as_expert():
        far = [(tie, core, 1, 4 + core), (tie_other, other, 4, 4 + other)]
        for c in (core, other):
            far += [(3, c, 3 * core, 2 + c), (-3, c, 5 - 3 * core, c)]
        near = []
        for o in (2, -2, 1, -1):
            for c in (core, other):
                near.append((o, c, 13 + o - 5 * core, 10 + 2 * o + c))
        near.append((0, other, 13 - 5 * core, 10 + other))
        return far, near

    def there(off, c, q, k, target):
        return remote(send.at[q], recv.at[k], s1.at[q], r1.at[k], target)

    def back(off, c, q, k, target):
        return remote(rsend.at[k], rrecv.at[q], s2.at[k], r2.at[q], target)

    def towards(e):
        return at_z(e[0], e[1])

    def whence(e):
        return at_z(-e[0], e[1])

    mine_q, mine_k = 13 - 5 * core, 10 + core
    src_far, src_near = as_source()
    exp_far, exp_near = as_expert()

    outs = []
    for first, count, group in ((0, FAR, src_far), (FAR, NEAR, src_near)):
        place = placing(first, count)

        @pl.loop(0, 4)
        def _(n):
            cols = ds(n * 256, 256)
            send[first : first + count, :, cols] = (
                dot(place, z[:, cols]).astype(BF16).reshape(count, BLK, 256)
            )

        for e in group:
            c = there(*e, towards(e))
            c.start()
            outs.append(c)
    self_out = pltpu.make_async_copy(send.at[mine_q], recv.at[mine_k], loc_sem.at[9])
    self_out.start()

    @pl.when(core == 1)
    def _():
        started = list(wz)

        def go(c):
            c.start()
            started.append(c)

        def y_slice(m, y):
            if m == 0:
                return wg.at[ds(y * (NX * GROWS), NX * GROWS), ALL]
            if m == 1:
                return wu.at[ds(px * (NY * GROWS) + y * GROWS, GROWS), ALL]
            return wd.at[ds(y * DROWS, DROWS), ds(px * QCOL, QCOL)]

        depth = ((4, 3), (3, 4), (3, 4))

        def chain(m, step):
            ss, rs = (gys, gyr) if m == 0 else (uys.at[m - 1], uyr.at[m - 1])
            for side, sign in ((0, 1), (1, -1)):
                if step > depth[m][side]:
                    continue
                w = y_slice(m, mod(py - sign * step, NY))
                if step > 0:
                    remote(w, w, ss.at[side, step - 1], rs.at[side, step - 1],
                           at_y(sign)).wait_recv()
                if step < depth[m][side]:
                    go(remote(w, w, ss.at[side, step], rs.at[side, step], at_y(sign)))

        def x_block(m, xx, part=None):
            if m == 1:
                n = NY * GROWS
                if part is None:
                    return wu.at[ds(xx * n, n), ALL]
                return wu.at[ds(xx * n + part * (n // 2), n // 2), ALL]
            rows = ALL if part is None else slice(part * MID, (part + 1) * MID)
            return wd.at[rows, ds(xx * QCOL, QCOL)]

        for m in (1, 2):
            wz[m].wait_recv()
            chain(m, 0)
        wz[0].wait_recv()
        w = wg.at[own[0]]
        for k in (2, 1, 3):
            go(remote(w, w, gxs.at[k - 1], gxr.at[k - 1], at_x(k)))
        for m in (1, 2):
            chain(m, 1)
        for k in (1, 3, 2):
            w = wg.at[ds(py * (NX * GROWS) + mod(px - k, NX) * GROWS, GROWS), ALL]
            remote(w, w, gxs.at[k - 1], gxr.at[k - 1], at_x(k)).wait_recv()
        chain(0, 0)
        for step in (2, 3, 4):
            for m in (1, 2):
                chain(m, step)
        for m in (1, 2):
            w = x_block(m, px)
            for side, sign in ((0, 1), (1, -1)):
                go(remote(w, w, uxs.at[m - 1, side, 0], uxr.at[m - 1, side, 0], at_x(sign)))
        chain(0, 1)
        for m in (1, 2):
            for side, sign in ((0, 1), (1, -1)):
                w = x_block(m, mod(px - sign, NX))
                remote(w, w, uxs.at[m - 1, side, 0], uxr.at[m - 1, side, 0],
                       at_x(sign)).wait_recv()
                w = x_block(m, mod(px - sign, NX), side)
                go(remote(w, w, uxs.at[m - 1, side, 1], uxr.at[m - 1, side, 1], at_x(sign)))
        for step in (2, 3, 4):
            chain(0, step)
        for m in (1, 2):
            for side, sign in ((0, 1), (1, -1)):
                w = x_block(m, mod(px + 2, NX), side)
                remote(w, w, uxs.at[m - 1, side, 1], uxr.at[m - 1, side, 1],
                       at_x(sign)).wait_recv()
        for c in started:
            c.wait_send()

    @pl.when(core == 0)
    def _():
        for c in wloads:
            c.wait()

    def gather_rows(first, count, pad, perm, dst):
        @pl.loop(0, 4)
        def _(n):
            cols = ds(n * 256, 256)
            rows = recv[first : first + count, :, cols].reshape(count * BLK, 256)
            dst[:, cols] = dot(perm[...], rows).astype(BF16)

        xl, xr = dst[0:pad, :], dst[pad : 2 * pad, :]
        dl, dr = dst[2 * pad : 3 * pad, :], dst[3 * pad :, :]
        a = dot(xl, wg[:HALF, :]) + dot(xr, wg[HALF:, :])
        b = dot(xl, wu[:HALF, :]) + dot(xr, wu[HALF:, :])
        dh = dot_nt(dl, wd[:, :HALF]) + dot_nt(dr, wd[:, HALF:])
        s = 1.0 / (1.0 + jnp.exp(-a))
        act = a * s
        hf = act * b
        da = (dh * b * s * (1.0 + a * (1.0 - s))).astype(BF16)
        db = (dh * act).astype(BF16)
        return hf, da, db

    def results(first, count, pad, perm_t, src, hf, da, db):
        h = hf.astype(BF16)
        for n in range(4):
            q, c0 = n // 2, QCOL * (n % 2)
            cols = slice(n * QCOL, (n + 1) * QCOL)
            src[q * pad : (q + 1) * pad, c0 : c0 + QCOL] = dot(h, wd[:, cols]).astype(BF16)
            grad = dot_nt(da, wg[cols, :]) + dot_nt(db, wu[cols, :])
            src[(2 + q) * pad : (3 + q) * pad, c0 : c0 + QCOL] = grad.astype(BF16)

        @pl.loop(0, 4)
        def _(n):
            cols = ds(n * 256, 256)
            rsend[first : first + count, :, cols] = (
                dot(perm_t[...], src[:, cols]).astype(BF16).reshape(count, BLK, 256)
            )

    backs = []
    for e in exp_far:
        there(*e, whence(e)).wait_recv()
    hf_far, da, db = gather_rows(0, FAR, FPAD, pf, xf)
    results(0, FAR, FPAD, pft, yf, hf_far, da, db)
    for e in exp_far:
        c = back(*e, whence(e))
        c.start()
        backs.append(c)

    self_out.wait()
    for e in exp_near:
        there(*e, whence(e)).wait_recv()
    hf, da, db = gather_rows(FAR, NEAR, NPAD, pn, xn)

    htf = jnp.transpose(hf_far).astype(BF16)
    htn = jnp.transpose(hf).astype(BF16)
    for j in range(NX):
        q, c0 = 2 + j // 2, QCOL * (j % 2)
        piece = dot(htf, xf[q * FPAD : (q + 1) * FPAD, c0 : c0 + QCOL])
        piece = piece + dot(htn, xn[q * NPAD : (q + 1) * NPAD, c0 : c0 + QCOL])
        dw[j] = piece
        dwb[j] = piece.astype(BF16)
    right, left, across = mod(px + 1, NX), mod(px - 1, NX), mod(px + 2, NX)
    lo, hi = slice(0, MID), slice(MID, FFW)
    dx_copies = [
        remote(dwb.at[across, lo], opp.at[0], dxs.at[0], dxr.at[0], at_x(1)),
        remote(dwb.at[across, hi], opp.at[1], dxs.at[1], dxr.at[1], at_x(-1)),
        remote(dwb.at[right, hi], pure.at[0], dxs.at[2], dxr.at[2], at_x(1)),
        remote(dwb.at[left, lo], pure.at[1], dxs.at[3], dxr.at[3], at_x(-1)),
    ]
    for c in dx_copies:
        c.start()

    results(FAR, NEAR, NPAD, pnt, yn, hf, da, db)
    for e in exp_near:
        c = back(*e, whence(e))
        c.start()
        backs.append(c)
    self_back = pltpu.make_async_copy(rsend.at[mine_k], rrecv.at[mine_q], loc_sem.at[10])
    self_back.start()

    merged = [
        remote(msend.at[0], mrecv.at[0], dxs.at[4], dxr.at[4], at_x(1)),
        remote(msend.at[1], mrecv.at[1], dxs.at[5], dxr.at[5], at_x(-1)),
    ]
    dx_copies[0].wait_recv()
    msend[0] = (dw[right, lo, :] + opp[0].astype(F32)).astype(BF16)
    merged[0].start()
    dx_copies[1].wait_recv()
    msend[1] = (dw[left, hi, :] + opp[1].astype(F32)).astype(BF16)
    merged[1].start()
    for c in dx_copies[2:] + merged:
        c.wait_recv()
    for i in range(NY):
        top = i < NY // 2
        rr = slice(i * DROWS, (i + 1) * DROWS)
        r0 = i * DROWS - (0 if top else MID)
        rm = slice(r0, r0 + DROWS)
        m, p = (0, 1) if top else (1, 0)
        part = dw[px, rr, :] + mrecv[m, rm, :].astype(F32) + pure[p, rm, :].astype(F32)
        ysum[i] = part
        yb[i] = part.astype(BF16)
    dy_copies = []
    for k in (4, 3, 5, 2, 6, 1, 7):
        c = remote(yb.at[mod(py + k, NY)], yrecv.at[k - 1], dys.at[k - 1], dyr.at[k - 1], at_y(k))
        c.start()
        dy_copies.append(c)
    for c in dy_copies:
        c.wait_recv()
    part = ysum[py]
    for k in range(NY - 1):
        part = part + yrecv[k].astype(F32)
    zsend[...] = part.astype(BF16)
    dz = remote(zsend, zrecv, dzs.at[0], dzr.at[0], at_z(8, other))

    @pl.when(core == 1)
    def _():
        dz.start()

    def taking(b, first, count):
        rows = slice(first * BLK, (first + count) * BLK)
        return jnp.where(wantc[b : b + 1, rows] == tgt_c, 1.0, 0.0).astype(BF16)

    takes = [taking(b, 0, FAR) for b in range(4)]
    for e in src_far:
        back(*e, towards(e)).wait_recv()
    for n in range(4):
        cols = slice(n * 256, (n + 1) * 256)
        src = rrecv[0:FAR, :, cols].reshape(FROWS, 256)
        for b in range(4):
            oacc[b, :, cols] = dot(takes[b], src)

    @pl.when(core == 0)
    def _():
        dz.wait_recv()
        total = part + zrecv[...].astype(F32)
        for i in range(2 * NX):
            fsend[i, 0:6, :] = total[i * 6 : (i + 1) * 6, :]
            fsend[i, 6:8, :] = jnp.zeros((2, QCOL), F32)
        mine = pltpu.make_async_copy(fsend.at[2 * px], frecv.at[px], loc_sem.at[11])
        mine.start()
        fins = [remote(fsend.at[2 * px + 1], frecv.at[px], fs.at[0, 1], fr.at[px],
                       dev(py, px, 1, pz))]
        for k in range(1, NX):
            to = mod(px + k, NX)
            for c in range(2):
                fins.append(
                    remote(fsend.at[2 * to + c], frecv.at[px], fs.at[k, c], fr.at[px],
                           dev(py, to, c, pz))
                )
        for c in fins:
            c.start()
        mine.wait()
        for k in range(1, NX):
            src = mod(px + k, NX)
            remote(fsend.at[0], frecv.at[src], fs.at[k, 0], fr.at[src],
                   dev(py, src, 0, pz)).wait_recv()
        for c in fins:
            c.wait_send()

    @pl.when(core == 1)
    def _():
        for src in range(NX):
            remote(fsend.at[0], frecv.at[src], fs.at[0, 0], fr.at[src],
                   dev(py, src, 0, pz)).wait_recv()
        dz.wait_send()

    for j in range(NX):
        for i in range(6):
            dgrad_ref[i, :, j * QCOL : (j + 1) * QCOL] = frecv[j, i : i + 1, :]

    takes = [taking(b, FAR, NEAR) for b in range(4)]
    self_back.wait()
    for e in src_near:
        back(*e, towards(e)).wait_recv()
    gsum = jnp.zeros((TOK, 1), F32)
    for n in range(4):
        cols = slice(n * 256, (n + 1) * 256)
        src = rrecv[FAR:, :, cols].reshape(NROWS, 256)
        for q in range(2):
            full = slice(q * HALF + n * 256, q * HALF + (n + 1) * 256)
            o = oacc[q, :, cols] + dot(takes[q], src)
            out_ref[:, full] = (gw_c * o).astype(BF16)
            gsum = gsum + jnp.sum(cot[:, full].astype(F32) * o, axis=1, keepdims=True)
            tgrad_ref[:, full] = (oacc[2 + q, :, cols] + dot(takes[2 + q], src)).astype(BF16)
    ggrad_ref[...] = jnp.sum(jnp.where(eye, gsum, 0.0), axis=0, keepdims=True)

    for c in outs + backs + dx_copies + merged + dy_copies:
        c.wait_send()


def hand_over(*refs):
    n = (len(refs) - 1) // 2
    copies = [
        pltpu.make_async_copy(refs[i], refs[n + i], refs[2 * n].at[i]) for i in range(n)
    ]
    for c in copies:
        c.start()
    for c in copies:
        c.wait()


def gathering(count, pad):
    perm = np.zeros((4 * pad, count * BLK), np.float32)
    for r in range(count * BLK):
        k, w = divmod(r, BLK)
        half, w = divmod(w, 2 * CAP)
        kind, s = divmod(w, CAP)
        perm[(kind * 2 + half) * pad + k * CAP + s, r] = 1.0
    return jnp.asarray(perm, BF16), jnp.asarray(perm.T, BF16)


def wanted():
    want = np.full((8, NZ * BLK), -1, np.int32)
    for r in range(NZ * BLK):
        k, w = divmod(r, BLK)
        half, w = divmod(w, 2 * CAP)
        kind, s = divmod(w, CAP)
        want[kind * 2 + half, r] = k * CAP + s
    return jnp.asarray(want)


def shards(tokens, expert_ids, gate_weights, cotangent, gate_weight, up_weight, down_weight):
    hbm = pl.BlockSpec(memory_space=pl.ANY)
    vmem = pl.BlockSpec(memory_space=pltpu.VMEM)
    dma = pltpu.SemaphoreType.DMA
    mem = pltpu.VMEM
    outs = (
        jax.ShapeDtypeStruct((TOK, WIDTH), BF16),
        jax.ShapeDtypeStruct((TOK, WIDTH), BF16),
        jax.ShapeDtypeStruct((1, TOK), F32),
        jax.ShapeDtypeStruct((FFW // (2 * NX * NY), 1, WIDTH), F32),
    )
    results = pl.pallas_call(
        kernel,
        out_shape=outs,
        in_specs=[hbm, hbm, vmem, vmem] + [hbm] * 7 + [vmem],
        out_specs=(vmem,) * 4,
        scratch_shapes=[
            mem((TOK, WIDTH), BF16), mem((TOK, WIDTH), BF16), mem((4 * TOK, HALF), BF16),
            mem((WIDTH, FFW), BF16), mem((WIDTH, FFW), BF16), mem((FFW, WIDTH), BF16),
            mem((4 * FPAD, FROWS), BF16), mem((FROWS, 4 * FPAD), BF16),
            mem((4 * NPAD, NROWS), BF16), mem((NROWS, 4 * NPAD), BF16),
            mem((NZ, BLK, HALF), BF16), mem((NZ, BLK, HALF), BF16),
            mem((4 * FPAD, HALF), BF16), mem((4 * FPAD, HALF), BF16),
            mem((4 * NPAD, HALF), BF16), mem((4 * NPAD, HALF), BF16),
            mem((NZ, BLK, HALF), BF16), mem((NZ, BLK, HALF), BF16),
            mem((4, TOK, HALF), F32),
            mem((NX, FFW, QCOL), F32), mem((NX, FFW, QCOL), BF16),
            mem((2, MID, QCOL), BF16), mem((2, MID, QCOL), BF16),
            mem((2, MID, QCOL), BF16), mem((2, MID, QCOL), BF16),
            mem((NY, DROWS, QCOL), F32), mem((NY, DROWS, QCOL), BF16),
            mem((NY - 1, DROWS, QCOL), BF16),
            mem((DROWS, QCOL), BF16), mem((DROWS, QCOL), BF16),
            mem((2 * NX, 8, QCOL), F32), mem((NX, 8, QCOL), F32),
            dma((12,)),
            dma((NZ,)), dma((NZ,)), dma((NZ,)), dma((NZ,)),
            dma((3,)), dma((3,)), dma((3,)), dma((3,)),
            dma((2, 4)), dma((2, 4)), dma((2, 2, 4)), dma((2, 2, 4)),
            dma((2, 2, 2)), dma((2, 2, 2)),
            dma((6,)), dma((6,)), dma((NY - 1,)), dma((NY - 1,)),
            dma((1,)), dma((1,)), dma((NX, 2)), dma((NX,)),
        ],
        compiler_params=pltpu.CompilerParams(
            collective_id=0, has_side_effects=True, vmem_limit_bytes=56 * 1024 * 1024
        ),
        cost_estimate=pl.CostEstimate(
            flops=6_000_000_000, bytes_accessed=16_000_000, transcendentals=100_000
        ),
    )(
        tokens, cotangent, expert_ids.reshape(1, TOK), gate_weights.reshape(1, TOK),
        gate_weight[0], up_weight[0], down_weight[0],
        *gathering(FAR, FPAD), *gathering(NEAR, NPAD), wanted(),
    )
    out, tgrad, ggrad, dgrad = pl.pallas_call(
        hand_over,
        out_shape=outs,
        in_specs=[hbm] * 4,
        out_specs=(hbm,) * 4,
        scratch_shapes=[dma((4,))],
        cost_estimate=pl.CostEstimate(flops=0, bytes_accessed=2_200_000, transcendentals=0),
    )(*results)
    return out, tgrad, ggrad.reshape(TOK, 1), jnp.transpose(dgrad, (1, 0, 2))


def solution(mesh):
    rows = P(("rep", "ep"), None)
    weight = P("ep", None, None)
    return jax.shard_map(
        shards,
        mesh=mesh,
        in_specs=(rows, rows, rows, rows, weight, weight, weight),
        out_specs=(rows, rows, rows, P("ep", "rep", None)),
        check_vma=False,
    )
```

```python
import jax
import jax.numpy as jnp
import numpy as np
from jax import lax
from jax.experimental import pallas as pl
from jax.experimental.pallas import tpu as pltpu
from jax.sharding import PartitionSpec as P

NX, NY, NZ = 4, 8, 16
TOK, WIDTH, FFW = 128, 2048, 384
CAP = 12
HALF = WIDTH // 2
BLK = 4 * CAP
FAR = 6
NEAR = NZ - FAR
FROWS, NROWS = FAR * BLK, NEAR * BLK
FPAD, NPAD = 80, 128
GROWS = WIDTH // (NX * NY)
DROWS = FFW // NY
QCOL = WIDTH // NX
MID = FFW // 2
GCOL = QCOL // 2
MESH = pl.DeviceIdType.MESH
F32 = jnp.float32
BF16 = jnp.bfloat16
NT = (((1,), (1,)), ((), ()))
ALL = slice(None)


def dot(a, b):
    return jnp.dot(a, b, preferred_element_type=F32)


def dot_nt(a, b):
    return lax.dot_general(a, b, NT, preferred_element_type=F32)


def ds(start, size):
    return pl.ds(pl.multiple_of(start, size), size)


def kernel(
    x_hbm, cot_hbm, ids_row, gw_row, wg_hbm, wu_hbm, wd_hbm, pf_hbm, pft_hbm, pn_hbm, pnt_hbm,
    wantc,
    out_ref, tgrad_ref, ggrad_ref, dgrad_ref,
    x, cot, z, wg, wu, wd, pf, pft, pn, pnt, send, recv, xf, yf, xn, yn, rsend, rrecv,
    oacc, dw, dwb, opp, pure, msend, mrecv, ysum, yb, yrecv, zsend, zrecv, fsend, frecv,
    loc_sem, s1, r1, s2, r2, wzs, wzr, gxs, gxr, gys, gyr, uys, uyr, uxs, uxr,
    dxs, dxr, dys, dyr, dzs, dzr, fs, fr,
):
    rep = lax.axis_index("rep")
    pz = lax.axis_index("ep")
    core = lax.rem(rep, 2)
    px = lax.rem(rep // 2, NX)
    py = rep // (2 * NX)
    other = 1 - core

    def dev(y, x_, c, z_):
        return ((y * NX + x_) * 2 + c, z_)

    def mod(v, n):
        return lax.rem(v + n, n)

    def at_x(k):
        return dev(py, mod(px + k, NX), core, pz)

    def at_y(k):
        return dev(mod(py + k, NY), px, core, pz)

    def at_z(off, c):
        return dev(py, px, c, mod(pz + off, NZ))

    def remote(src, dst, ss, rs, target):
        return pltpu.make_async_remote_copy(
            src_ref=src, dst_ref=dst, send_sem=ss, recv_sem=rs,
            device_id=target, device_id_type=MESH,
        )

    tie, tie_other = 4 - 8 * core, 4 - 8 * other
    barrier = pltpu.get_barrier_semaphore()
    peers = [at_z(o, core) for o in (-4, -3, -2, -1, 1, 2, 3, 4, 8)]
    peers += [at_z(o, other) for o in (-3, -2, -1, 0, 1, 2, 3, 8)] + [at_z(tie, other)]
    for k in range(1, NX):
        peers.append(at_x(k))
        peers.append(dev(py, mod(px + k, NX), other, pz))
    for k in range(1, NY):
        peers.append(at_y(k))
    for peer in peers:
        pl.semaphore_signal(barrier, inc=1, device_id=peer, device_id_type=MESH)

    loads = [
        pltpu.make_async_copy(s, d, loc_sem.at[i])
        for i, (s, d) in enumerate(
            ((x_hbm, x), (cot_hbm, cot), (pf_hbm, pf), (pft_hbm, pft), (pn_hbm, pn), (pnt_hbm, pnt))
        )
    ]
    for c in loads:
        c.start()
    weights = (wg, wu, wd)
    wloads = [
        pltpu.make_async_copy(s, d, loc_sem.at[6 + i])
        for i, (s, d) in enumerate(zip((wg_hbm, wu_hbm, wd_hbm), weights))
    ]

    @pl.when(core == 0)
    def _():
        for c in wloads:
            c.start()

    def place_of(ids):
        u = lax.rem(ids - pz + (2 * NZ - 3), NZ)
        u = u + jnp.where((u >= 3) & (u < 8), 3, 0) - jnp.where((u >= 8) & (u < 11), 5, 0)
        return u

    lane = lax.broadcasted_iota(jnp.int32, (TOK, TOK), 1)
    sub = lax.broadcasted_iota(jnp.int32, (TOK, TOK), 0)
    eye = lane == sub
    q_r = place_of(ids_row[...])
    q_c = jnp.sum(jnp.where(eye, q_r, 0), axis=1, keepdims=True)
    gw_c = jnp.sum(jnp.where(eye, gw_row[...], 0.0), axis=1, keepdims=True)
    oh_r = (lax.broadcasted_iota(jnp.int32, (NZ, TOK), 0) == q_r).astype(F32)
    before = dot(oh_r.astype(BF16), (sub < lane).astype(F32).astype(BF16))
    slot_r = jnp.sum(before * oh_r, axis=0, keepdims=True).astype(jnp.int32)
    tgt_r = q_r * CAP + slot_r
    tgt_c = jnp.sum(jnp.where(eye, tgt_r, 0), axis=1, keepdims=True)

    def placing(first, count):
        ex = lax.broadcasted_iota(jnp.int32, (count, BLK, TOK), 0) + first
        row = lax.broadcasted_iota(jnp.int32, (count, BLK, TOK), 1)
        half = jnp.where(row >= 2 * CAP, 1, 0)
        row = row - 2 * CAP * half
        kind = jnp.where(row >= CAP, 1, 0)
        want = ex * CAP + row - CAP * kind
        quarter = jnp.where(want == tgt_r.reshape(1, 1, TOK), kind * 2 + half, -1)
        return jnp.concatenate(
            [
                jnp.where(quarter == b, 1.0, 0.0).reshape(count * BLK, TOK).astype(BF16)
                for b in range(4)
            ],
            axis=1,
        )

    for c in loads:
        c.wait()
    z[0:TOK, :] = x[:, :HALF]
    z[TOK : 2 * TOK, :] = x[:, HALF:]
    dout = (gw_c * cot[...].astype(F32)).astype(BF16)
    z[2 * TOK : 3 * TOK, :] = dout[:, :HALF]
    z[3 * TOK :, :] = dout[:, HALF:]

    def build(first, count):
        place = placing(first, count)

        @pl.loop(0, 4)
        def _(n):
            cols = ds(n * 256, 256)
            send[first : first + count, :, cols] = (
                dot(place, z[:, cols]).astype(BF16).reshape(count, BLK, 256)
            )

    build(0, FAR)
    pl.semaphore_wait(barrier, len(peers))

    own = (
        (ds(py * (NX * GROWS) + px * GROWS, GROWS), ALL),
        (ds(px * (NY * GROWS) + py * GROWS, GROWS), ALL),
        (ds(py * DROWS, DROWS), ds(px * QCOL, QCOL)),
    )
    wz = [
        remote(h.at[i], w.at[i], wzs.at[m], wzr.at[m], at_z(8, core))
        for m, (h, w, i) in enumerate(zip((wg_hbm, wu_hbm, wd_hbm), weights, own))
    ]

    @pl.when(core == 1)
    def _():
        for m in (1, 2, 0):
            wz[m].start()

    def as_source():
        far = [(tie, core, 1, 4 + core), (tie, other, 4, 4 + core)]
        for c in (core, other):
            far += [(3, c, 3 * c, 2 + core), (-3, c, 5 - 3 * c, core)]
        near = []
        for o in (2, -2, 1, -1):
            for c in (core, other):
                near.append((o, c, 13 + o - 5 * c, 10 + 2 * o + core))
        near.append((0, other, 13 - 5 * other, 10 + core))
        return far, near

    def as_expert():
        far = [(tie, core, 1, 4 + core), (tie_other, other, 4, 4 + other)]
        for c in (core, other):
            far += [(3, c, 3 * core, 2 + c), (-3, c, 5 - 3 * core, c)]
        near = []
        for o in (2, -2, 1, -1):
            for c in (core, other):
                near.append((o, c, 13 + o - 5 * core, 10 + 2 * o + c))
        near.append((0, other, 13 - 5 * core, 10 + other))
        return far, near

    def there(off, c, q, k, target):
        return remote(send.at[q], recv.at[k], s1.at[q], r1.at[k], target)

    def back(off, c, q, k, target):
        return remote(rsend.at[k], rrecv.at[q], s2.at[k], r2.at[q], target)

    def towards(e):
        return at_z(e[0], e[1])

    def whence(e):
        return at_z(-e[0], e[1])

    mine_q, mine_k = 13 - 5 * core, 10 + core
    src_far, src_near = as_source()
    exp_far, exp_near = as_expert()

    outs = [there(*e, towards(e)) for e in src_far]
    for c in outs:
        c.start()
    build(FAR, NEAR)
    for e in src_near:
        c = there(*e, towards(e))
        c.start()
        outs.append(c)
    self_out = pltpu.make_async_copy(send.at[mine_q], recv.at[mine_k], loc_sem.at[9])
    self_out.start()

    @pl.when(core == 1)
    def _():
        started = list(wz)

        def go(c):
            c.start()
            started.append(c)

        def y_slice(m, y):
            if m == 0:
                return wg.at[ds(y * (NX * GROWS), NX * GROWS), ALL]
            if m == 1:
                return wu.at[ds(px * (NY * GROWS) + y * GROWS, GROWS), ALL]
            return wd.at[ds(y * DROWS, DROWS), ds(px * QCOL, QCOL)]

        depth = ((4, 3), (3, 4), (3, 4))

        def chain(m, step):
            ss, rs = (gys, gyr) if m == 0 else (uys.at[m - 1], uyr.at[m - 1])
            for side, sign in ((0, 1), (1, -1)):
                if step > depth[m][side]:
                    continue
                w = y_slice(m, mod(py - sign * step, NY))
                if step > 0:
                    remote(w, w, ss.at[side, step - 1], rs.at[side, step - 1],
                           at_y(sign)).wait_recv()
                if step < depth[m][side]:
                    go(remote(w, w, ss.at[side, step], rs.at[side, step], at_y(sign)))

        def x_block(m, xx, part=None):
            if m == 1:
                n = NY * GROWS
                if part is None:
                    return wu.at[ds(xx * n, n), ALL]
                return wu.at[ds(xx * n + part * (n // 2), n // 2), ALL]
            rows = ALL if part is None else slice(part * MID, (part + 1) * MID)
            return wd.at[rows, ds(xx * QCOL, QCOL)]

        for m in (1, 2):
            wz[m].wait_recv()
            chain(m, 0)
        wz[0].wait_recv()
        w = wg.at[own[0]]
        for k in (2, 1, 3):
            go(remote(w, w, gxs.at[k - 1], gxr.at[k - 1], at_x(k)))
        for m in (1, 2):
            chain(m, 1)
        for k in (1, 3, 2):
            w = wg.at[ds(py * (NX * GROWS) + mod(px - k, NX) * GROWS, GROWS), ALL]
            remote(w, w, gxs.at[k - 1], gxr.at[k - 1], at_x(k)).wait_recv()
        chain(0, 0)
        for step in (2, 3, 4):
            for m in (1, 2):
                chain(m, step)
        for m in (1, 2):
            w = x_block(m, px)
            for side, sign in ((0, 1), (1, -1)):
                go(remote(w, w, uxs.at[m - 1, side, 0], uxr.at[m - 1, side, 0], at_x(sign)))
        chain(0, 1)
        for m in (1, 2):
            for side, sign in ((0, 1), (1, -1)):
                w = x_block(m, mod(px - sign, NX))
                remote(w, w, uxs.at[m - 1, side, 0], uxr.at[m - 1, side, 0],
                       at_x(sign)).wait_recv()
                w = x_block(m, mod(px - sign, NX), side)
                go(remote(w, w, uxs.at[m - 1, side, 1], uxr.at[m - 1, side, 1], at_x(sign)))
        for step in (2, 3, 4):
            chain(0, step)
        for m in (1, 2):
            for side, sign in ((0, 1), (1, -1)):
                w = x_block(m, mod(px + 2, NX), side)
                remote(w, w, uxs.at[m - 1, side, 1], uxr.at[m - 1, side, 1],
                       at_x(sign)).wait_recv()
        for c in started:
            c.wait_send()

    @pl.when(core == 0)
    def _():
        for c in wloads:
            c.wait()

    def gather_rows(first, count, pad, perm, dst):
        @pl.loop(0, 4)
        def _(n):
            cols = ds(n * 256, 256)
            rows = recv[first : first + count, :, cols].reshape(count * BLK, 256)
            dst[:, cols] = dot(perm[...], rows).astype(BF16)

        xl, xr = dst[0:pad, :], dst[pad : 2 * pad, :]
        dl, dr = dst[2 * pad : 3 * pad, :], dst[3 * pad :, :]
        a = dot(xl, wg[:HALF, :]) + dot(xr, wg[HALF:, :])
        b = dot(xl, wu[:HALF, :]) + dot(xr, wu[HALF:, :])
        dh = dot_nt(dl, wd[:, :HALF]) + dot_nt(dr, wd[:, HALF:])
        s = 1.0 / (1.0 + jnp.exp(-a))
        act = a * s
        hf = act * b
        da = (dh * b * s * (1.0 + a * (1.0 - s))).astype(BF16)
        db = (dh * act).astype(BF16)
        return hf, da, db

    def results(first, count, pad, perm_t, src, hf, da, db):
        h = hf.astype(BF16)
        for n in range(4):
            q, c0 = n // 2, QCOL * (n % 2)
            cols = slice(n * QCOL, (n + 1) * QCOL)
            src[q * pad : (q + 1) * pad, c0 : c0 + QCOL] = dot(h, wd[:, cols]).astype(BF16)
            grad = dot_nt(da, wg[cols, :]) + dot_nt(db, wu[cols, :])
            src[(2 + q) * pad : (3 + q) * pad, c0 : c0 + QCOL] = grad.astype(BF16)

        @pl.loop(0, 4)
        def _(n):
            cols = ds(n * 256, 256)
            rsend[first : first + count, :, cols] = (
                dot(perm_t[...], src[:, cols]).astype(BF16).reshape(count, BLK, 256)
            )

    backs = []
    for e in exp_far:
        there(*e, whence(e)).wait_recv()
    hf_far, da, db = gather_rows(0, FAR, FPAD, pf, xf)
    results(0, FAR, FPAD, pft, yf, hf_far, da, db)
    self_out.wait()
    for e in exp_near:
        there(*e, whence(e)).wait_recv()
    for e in exp_far:
        c = back(*e, whence(e))
        c.start()
        backs.append(c)
    hf, da, db = gather_rows(FAR, NEAR, NPAD, pn, xn)

    htf = jnp.transpose(hf_far).astype(BF16)
    htn = jnp.transpose(hf).astype(BF16)
    for j in range(NX):
        q, c0 = 2 + j // 2, QCOL * (j % 2)
        piece = dot(htf, xf[q * FPAD : (q + 1) * FPAD, c0 : c0 + QCOL])
        piece = piece + dot(htn, xn[q * NPAD : (q + 1) * NPAD, c0 : c0 + QCOL])
        dw[j] = piece
        for g in range(2):
            dwb[g, j] = piece[:, g * GCOL : (g + 1) * GCOL].astype(BF16)
    right, left, across = mod(px + 1, NX), mod(px - 1, NX), mod(px + 2, NX)
    lo, hi = slice(0, MID), slice(MID, FFW)
    dx_copies = []
    for g in range(2):
        for i, (to, rr, side) in enumerate(
            ((across, lo, 1), (across, hi, -1), (right, hi, 1), (left, lo, -1))
        ):
            dst = (opp if i < 2 else pure).at[g, i % 2]
            c = remote(dwb.at[g, to, rr], dst, dxs.at[g, i], dxr.at[g, i], at_x(side))
            c.start()
            dx_copies.append(c)

    results(FAR, NEAR, NPAD, pnt, yn, hf, da, db)
    for e in exp_near:
        c = back(*e, whence(e))
        c.start()
        backs.append(c)
    self_back = pltpu.make_async_copy(rsend.at[mine_k], rrecv.at[mine_q], loc_sem.at[10])
    self_back.start()

    halves = [slice(g * GCOL, (g + 1) * GCOL) for g in range(2)]
    merged = []
    for g in range(2):
        for i, (to, rr, side) in enumerate(((right, lo, 1), (left, hi, -1))):
            dx_copies[4 * g + i].wait_recv()
            msend[g, i] = (dw[to, rr, halves[g]] + opp[g, i].astype(F32)).astype(BF16)
            c = remote(msend.at[g, i], mrecv.at[g, i], dxs.at[g, 4 + i], dxr.at[g, 4 + i],
                       at_x(side))
            c.start()
            merged.append(c)
    dy_copies = []
    for g in range(2):
        for c in dx_copies[4 * g + 2 : 4 * g + 4] + merged[2 * g : 2 * g + 2]:
            c.wait_recv()
        for i in range(NY):
            top = i < NY // 2
            rr = slice(i * DROWS, (i + 1) * DROWS)
            r0 = i * DROWS - (0 if top else MID)
            rm = slice(r0, r0 + DROWS)
            m, p = (0, 1) if top else (1, 0)
            got = mrecv[g, m, rm, :].astype(F32) + pure[g, p, rm, :].astype(F32)
            got = dw[px, rr, halves[g]] + got
            ysum[i, :, halves[g]] = got
            yb[g, i] = got.astype(BF16)
        for k in (4, 3, 5, 2, 6, 1, 7):
            c = remote(yb.at[g, mod(py + k, NY)], yrecv.at[g, k - 1], dys.at[g, k - 1],
                       dyr.at[g, k - 1], at_y(k))
            c.start()
            dy_copies.append(c)
    sums = []
    for g in range(2):
        for c in dy_copies[g * (NY - 1) : (g + 1) * (NY - 1)]:
            c.wait_recv()
        got = ysum[py, :, halves[g]]
        for k in range(NY - 1):
            got = got + yrecv[g, k].astype(F32)
        sums.append(got)
    part = jnp.concatenate(sums, axis=1)
    zsend[...] = part.astype(BF16)
    dz = remote(zsend, zrecv, dzs.at[0], dzr.at[0], at_z(8, other))

    @pl.when(core == 1)
    def _():
        dz.start()

    def taking(b, first, count):
        rows = slice(first * BLK, (first + count) * BLK)
        return jnp.where(wantc[b : b + 1, rows] == tgt_c, 1.0, 0.0).astype(BF16)

    takes = [taking(b, 0, FAR) for b in range(4)]
    for e in src_far:
        back(*e, towards(e)).wait_recv()
    for n in range(4):
        cols = slice(n * 256, (n + 1) * 256)
        src = rrecv[0:FAR, :, cols].reshape(FROWS, 256)
        for b in range(4):
            oacc[b, :, cols] = dot(takes[b], src)

    @pl.when(core == 0)
    def _():
        dz.wait_recv()
        total = part + zrecv[...].astype(F32)
        for i in range(2 * NX):
            fsend[i, 0:6, :] = total[i * 6 : (i + 1) * 6, :]
            fsend[i, 6:8, :] = jnp.zeros((2, QCOL), F32)
        mine = pltpu.make_async_copy(fsend.at[2 * px], frecv.at[px], loc_sem.at[11])
        mine.start()
        fins = [remote(fsend.at[2 * px + 1], frecv.at[px], fs.at[0, 1], fr.at[px],
                       dev(py, px, 1, pz))]
        for k in range(1, NX):
            to = mod(px + k, NX)
            for c in range(2):
                fins.append(
                    remote(fsend.at[2 * to + c], frecv.at[px], fs.at[k, c], fr.at[px],
                           dev(py, to, c, pz))
                )
        for c in fins:
            c.start()
        mine.wait()
        for k in range(1, NX):
            src = mod(px + k, NX)
            remote(fsend.at[0], frecv.at[src], fs.at[k, 0], fr.at[src],
                   dev(py, src, 0, pz)).wait_recv()
        for c in fins:
            c.wait_send()

    @pl.when(core == 1)
    def _():
        for src in range(NX):
            remote(fsend.at[0], frecv.at[src], fs.at[0, 0], fr.at[src],
                   dev(py, src, 0, pz)).wait_recv()
        dz.wait_send()

    for j in range(NX):
        for i in range(6):
            dgrad_ref[i, :, j * QCOL : (j + 1) * QCOL] = frecv[j, i : i + 1, :]

    takes = [taking(b, FAR, NEAR) for b in range(4)]
    self_back.wait()
    for e in src_near:
        back(*e, towards(e)).wait_recv()
    gsum = jnp.zeros((TOK, 1), F32)
    for n in range(4):
        cols = slice(n * 256, (n + 1) * 256)
        src = rrecv[FAR:, :, cols].reshape(NROWS, 256)
        for q in range(2):
            full = slice(q * HALF + n * 256, q * HALF + (n + 1) * 256)
            o = oacc[q, :, cols] + dot(takes[q], src)
            out_ref[:, full] = (gw_c * o).astype(BF16)
            gsum = gsum + jnp.sum(cot[:, full].astype(F32) * o, axis=1, keepdims=True)
            tgrad_ref[:, full] = (oacc[2 + q, :, cols] + dot(takes[2 + q], src)).astype(BF16)
    ggrad_ref[...] = jnp.sum(jnp.where(eye, gsum, 0.0), axis=0, keepdims=True)

    for c in outs + backs + dx_copies + merged + dy_copies:
        c.wait_send()


def hand_over(*refs):
    n = len(refs) // 2
    for i in range(n):
        refs[n + i][...] = refs[i][...]


def gathering(count, pad):
    perm = np.zeros((4 * pad, count * BLK), np.float32)
    for r in range(count * BLK):
        k, w = divmod(r, BLK)
        half, w = divmod(w, 2 * CAP)
        kind, s = divmod(w, CAP)
        perm[(kind * 2 + half) * pad + k * CAP + s, r] = 1.0
    return jnp.asarray(perm, BF16), jnp.asarray(perm.T, BF16)


def wanted():
    want = np.full((8, NZ * BLK), -1, np.int32)
    for r in range(NZ * BLK):
        k, w = divmod(r, BLK)
        half, w = divmod(w, 2 * CAP)
        kind, s = divmod(w, CAP)
        want[kind * 2 + half, r] = k * CAP + s
    return jnp.asarray(want)


def shards(tokens, expert_ids, gate_weights, cotangent, gate_weight, up_weight, down_weight):
    hbm = pl.BlockSpec(memory_space=pl.ANY)
    vmem = pl.BlockSpec(memory_space=pltpu.VMEM)
    dma = pltpu.SemaphoreType.DMA
    mem = pltpu.VMEM
    outs = (
        jax.ShapeDtypeStruct((TOK, WIDTH), BF16),
        jax.ShapeDtypeStruct((TOK, WIDTH), BF16),
        jax.ShapeDtypeStruct((1, TOK), F32),
        jax.ShapeDtypeStruct((FFW // (2 * NX * NY), 1, WIDTH), F32),
    )
    results = pl.pallas_call(
        kernel,
        out_shape=outs,
        in_specs=[hbm, hbm, vmem, vmem] + [hbm] * 7 + [vmem],
        out_specs=(vmem,) * 4,
        scratch_shapes=[
            mem((TOK, WIDTH), BF16), mem((TOK, WIDTH), BF16), mem((4 * TOK, HALF), BF16),
            mem((WIDTH, FFW), BF16), mem((WIDTH, FFW), BF16), mem((FFW, WIDTH), BF16),
            mem((4 * FPAD, FROWS), BF16), mem((FROWS, 4 * FPAD), BF16),
            mem((4 * NPAD, NROWS), BF16), mem((NROWS, 4 * NPAD), BF16),
            mem((NZ, BLK, HALF), BF16), mem((NZ, BLK, HALF), BF16),
            mem((4 * FPAD, HALF), BF16), mem((4 * FPAD, HALF), BF16),
            mem((4 * NPAD, HALF), BF16), mem((4 * NPAD, HALF), BF16),
            mem((NZ, BLK, HALF), BF16), mem((NZ, BLK, HALF), BF16),
            mem((4, TOK, HALF), F32),
            mem((NX, FFW, QCOL), F32), mem((2, NX, FFW, GCOL), BF16),
            mem((2, 2, MID, GCOL), BF16), mem((2, 2, MID, GCOL), BF16),
            mem((2, 2, MID, GCOL), BF16), mem((2, 2, MID, GCOL), BF16),
            mem((NY, DROWS, QCOL), F32), mem((2, NY, DROWS, GCOL), BF16),
            mem((2, NY - 1, DROWS, GCOL), BF16),
            mem((DROWS, QCOL), BF16), mem((DROWS, QCOL), BF16),
            mem((2 * NX, 8, QCOL), F32), mem((NX, 8, QCOL), F32),
            dma((12,)),
            dma((NZ,)), dma((NZ,)), dma((NZ,)), dma((NZ,)),
            dma((3,)), dma((3,)), dma((3,)), dma((3,)),
            dma((2, 4)), dma((2, 4)), dma((2, 2, 4)), dma((2, 2, 4)),
            dma((2, 2, 2)), dma((2, 2, 2)),
            dma((2, 6)), dma((2, 6)), dma((2, NY - 1)), dma((2, NY - 1)),
            dma((1,)), dma((1,)), dma((NX, 2)), dma((NX,)),
        ],
        compiler_params=pltpu.CompilerParams(
            collective_id=0, has_side_effects=True, vmem_limit_bytes=56 * 1024 * 1024
        ),
        cost_estimate=pl.CostEstimate(
            flops=6_000_000_000, bytes_accessed=16_000_000, transcendentals=100_000
        ),
    )(
        tokens, cotangent, expert_ids.reshape(1, TOK), gate_weights.reshape(1, TOK),
        gate_weight[0], up_weight[0], down_weight[0],
        *gathering(FAR, FPAD), *gathering(NEAR, NPAD), wanted(),
    )
    out, tgrad, ggrad, dgrad = pl.pallas_call(
        hand_over,
        out_shape=outs,
        in_specs=[vmem] * 4,
        out_specs=(vmem,) * 4,
        cost_estimate=pl.CostEstimate(flops=0, bytes_accessed=2_200_000, transcendentals=0),
    )(*results)
    return out, tgrad, ggrad.reshape(TOK, 1), jnp.transpose(dgrad, (1, 0, 2))


def solution(mesh):
    rows = P(("rep", "ep"), None)
    weight = P("ep", None, None)
    return jax.shard_map(
        shards,
        mesh=mesh,
        in_specs=(rows, rows, rows, rows, weight, weight, weight),
        out_specs=(rows, rows, rows, P("ep", "rep", None)),
        check_vma=False,
    )
```

```python
import jax
import jax.numpy as jnp
import numpy as np
from jax import lax
from jax.experimental import pallas as pl
from jax.experimental.pallas import tpu as pltpu
from jax.sharding import PartitionSpec as P

NX, NY, NZ = 4, 8, 16
TOK, WIDTH, FFW = 128, 2048, 384
CAP = 12
HALF = WIDTH // 2
BLK = 4 * CAP
FAR = 6
NEAR = NZ - FAR
FROWS, NROWS = FAR * BLK, NEAR * BLK
FPAD, NPAD = 80, 128
GROWS = WIDTH // (NX * NY)
DROWS = FFW // NY
QCOL = WIDTH // NX
MID = FFW // 2
GCOL = QCOL // 2
MESH = pl.DeviceIdType.MESH
F32 = jnp.float32
BF16 = jnp.bfloat16
NT = (((1,), (1,)), ((), ()))
ALL = slice(None)


def dot(a, b):
    return jnp.dot(a, b, preferred_element_type=F32)


def dot_nt(a, b):
    return lax.dot_general(a, b, NT, preferred_element_type=F32)


def ds(start, size):
    return pl.ds(pl.multiple_of(start, size), size)


def kernel(
    x_hbm, cot_hbm, ids_row, gw_row, wg_hbm, wu_hbm, wd_hbm, pf_hbm, pft_hbm, pn_hbm, pnt_hbm,
    wantc,
    out_ref, tgrad_ref, ggrad_ref, dgrad_ref,
    x, cot, z, wg, wu, wd, pf, pft, pn, pnt, send, recv, xf, yf, xn, yn, rsend, rrecv,
    oacc, dw, dwb, opp, pure, msend, mrecv, ysum, yb, yrecv, zsend, zrecv, fsend, frecv,
    loc_sem, s1, r1, s2, r2, wzs, wzr, gxs, gxr, gys, gyr, uys, uyr, uxs, uxr,
    dxs, dxr, dys, dyr, dzs, dzr, fs, fr, go_sem,
):
    rep = lax.axis_index("rep")
    pz = lax.axis_index("ep")
    core = lax.rem(rep, 2)
    px = lax.rem(rep // 2, NX)
    py = rep // (2 * NX)
    other = 1 - core

    def dev(y, x_, c, z_):
        return ((y * NX + x_) * 2 + c, z_)

    def mod(v, n):
        return lax.rem(v + n, n)

    def at_x(k):
        return dev(py, mod(px + k, NX), core, pz)

    def at_y(k):
        return dev(mod(py + k, NY), px, core, pz)

    def at_z(off, c):
        return dev(py, px, c, mod(pz + off, NZ))

    def remote(src, dst, ss, rs, target):
        return pltpu.make_async_remote_copy(
            src_ref=src, dst_ref=dst, send_sem=ss, recv_sem=rs,
            device_id=target, device_id_type=MESH,
        )

    tie, tie_other = 4 - 8 * core, 4 - 8 * other
    barrier = pltpu.get_barrier_semaphore()
    peers = [at_z(o, core) for o in (-4, -3, -2, -1, 1, 2, 3, 4, 8)]
    peers += [at_z(o, other) for o in (-3, -2, -1, 0, 1, 2, 3, 8)] + [at_z(tie, other)]
    for k in range(1, NX):
        peers.append(at_x(k))
        peers.append(dev(py, mod(px + k, NX), other, pz))
    for k in range(1, NY):
        peers.append(at_y(k))
    for peer in peers:
        pl.semaphore_signal(barrier, inc=1, device_id=peer, device_id_type=MESH)

    loads = [
        pltpu.make_async_copy(s, d, loc_sem.at[i])
        for i, (s, d) in enumerate(
            ((x_hbm, x), (cot_hbm, cot), (pf_hbm, pf), (pft_hbm, pft), (pn_hbm, pn), (pnt_hbm, pnt))
        )
    ]
    for c in loads:
        c.start()
    weights = (wg, wu, wd)
    wloads = [
        pltpu.make_async_copy(s, d, loc_sem.at[6 + i])
        for i, (s, d) in enumerate(zip((wg_hbm, wu_hbm, wd_hbm), weights))
    ]

    @pl.when(core == 0)
    def _():
        for c in wloads:
            c.start()

    def place_of(ids):
        u = lax.rem(ids - pz + (2 * NZ - 3), NZ)
        u = u + jnp.where((u >= 3) & (u < 8), 3, 0) - jnp.where((u >= 8) & (u < 11), 5, 0)
        return u

    lane = lax.broadcasted_iota(jnp.int32, (TOK, TOK), 1)
    sub = lax.broadcasted_iota(jnp.int32, (TOK, TOK), 0)
    eye = lane == sub
    q_r = place_of(ids_row[...])
    q_c = jnp.sum(jnp.where(eye, q_r, 0), axis=1, keepdims=True)
    gw_c = jnp.sum(jnp.where(eye, gw_row[...], 0.0), axis=1, keepdims=True)
    oh_r = (lax.broadcasted_iota(jnp.int32, (NZ, TOK), 0) == q_r).astype(F32)
    before = dot(oh_r.astype(BF16), (sub < lane).astype(F32).astype(BF16))
    slot_r = jnp.sum(before * oh_r, axis=0, keepdims=True).astype(jnp.int32)
    tgt_r = q_r * CAP + slot_r
    tgt_c = jnp.sum(jnp.where(eye, tgt_r, 0), axis=1, keepdims=True)

    def placing(first, count):
        ex = lax.broadcasted_iota(jnp.int32, (count, BLK, TOK), 0) + first
        row = lax.broadcasted_iota(jnp.int32, (count, BLK, TOK), 1)
        half = jnp.where(row >= 2 * CAP, 1, 0)
        row = row - 2 * CAP * half
        kind = jnp.where(row >= CAP, 1, 0)
        want = ex * CAP + row - CAP * kind
        quarter = jnp.where(want == tgt_r.reshape(1, 1, TOK), kind * 2 + half, -1)
        return jnp.concatenate(
            [
                jnp.where(quarter == b, 1.0, 0.0).reshape(count * BLK, TOK).astype(BF16)
                for b in range(4)
            ],
            axis=1,
        )

    place_far = placing(0, FAR)
    pl.semaphore_wait(barrier, len(peers))

    own = (
        (ds(py * (NX * GROWS) + px * GROWS, GROWS), ALL),
        (ds(px * (NY * GROWS) + py * GROWS, GROWS), ALL),
        (ds(py * DROWS, DROWS), ds(px * QCOL, QCOL)),
    )
    wz = [
        remote(h.at[i], w.at[i], wzs.at[m], wzr.at[m], at_z(8, core))
        for m, (h, w, i) in enumerate(zip((wg_hbm, wu_hbm, wd_hbm), weights, own))
    ]

    @pl.when(core == 1)
    def _():
        for m in (1, 2, 0):
            wz[m].start()

    for c in loads[:2]:
        c.wait()
    z[0:TOK, :] = x[:, :HALF]
    z[TOK : 2 * TOK, :] = x[:, HALF:]
    dout = (gw_c * cot[...].astype(F32)).astype(BF16)
    z[2 * TOK : 3 * TOK, :] = dout[:, :HALF]
    z[3 * TOK :, :] = dout[:, HALF:]

    def build(place, first, count):
        @pl.loop(0, 4)
        def _(n):
            cols = ds(n * 256, 256)
            send[first : first + count, :, cols] = (
                dot(place, z[:, cols]).astype(BF16).reshape(count, BLK, 256)
            )

    build(place_far, 0, FAR)

    def as_source():
        far = [(tie, core, 1, 4 + core), (tie, other, 4, 4 + core)]
        for c in (core, other):
            far += [(3, c, 3 * c, 2 + core), (-3, c, 5 - 3 * c, core)]
        near = []
        for o in (2, -2, 1, -1):
            for c in (core, other):
                near.append((o, c, 13 + o - 5 * c, 10 + 2 * o + core))
        near.append((0, other, 13 - 5 * other, 10 + core))
        return far, near

    def as_expert():
        far = [(tie, core, 1, 4 + core), (tie_other, other, 4, 4 + other)]
        for c in (core, other):
            far += [(3, c, 3 * core, 2 + c), (-3, c, 5 - 3 * core, c)]
        near = []
        for o in (2, -2, 1, -1):
            for c in (core, other):
                near.append((o, c, 13 + o - 5 * core, 10 + 2 * o + c))
        near.append((0, other, 13 - 5 * core, 10 + other))
        return far, near

    def there(off, c, q, k, target):
        return remote(send.at[q], recv.at[k], s1.at[q], r1.at[k], target)

    def back(off, c, q, k, target):
        return remote(rsend.at[k], rrecv.at[q], s2.at[k], r2.at[q], target)

    def towards(e):
        return at_z(e[0], e[1])

    def whence(e):
        return at_z(-e[0], e[1])

    mine_q, mine_k = 13 - 5 * core, 10 + core
    src_far, src_near = as_source()
    exp_far, exp_near = as_expert()

    outs = [there(*e, towards(e)) for e in src_far]
    for c in outs:
        c.start()
    build(placing(FAR, NEAR), FAR, NEAR)

    def y_slice(m, y):
        if m == 0:
            return wg.at[ds(y * (NX * GROWS), NX * GROWS), ALL]
        if m == 1:
            return wu.at[ds(px * (NY * GROWS) + y * GROWS, GROWS), ALL]
        return wd.at[ds(y * DROWS, DROWS), ds(px * QCOL, QCOL)]

    def first_copies(m):
        if m == 0:
            w = wg.at[own[0]]
            return [remote(w, w, gxs.at[k - 1], gxr.at[k - 1], at_x(k)) for k in (2, 1, 3)]
        w = y_slice(m, py)
        return [
            remote(w, w, uys.at[m - 1, k - 1], uyr.at[m - 1, k - 1], at_y(k))
            for k in (4, 3, 5, 2, 6, 1, 7)
        ]

    @pl.when(core == 1)
    def _():
        for m in (1, 2, 0):
            wz[m].wait_recv()
            for c in first_copies(m):
                c.start()
        pl.semaphore_signal(go_sem, inc=1, device_id=at_z(0, other), device_id_type=MESH)

    @pl.when(core == 0)
    def _():
        pl.semaphore_wait(go_sem, 1)

    for e in src_near:
        c = there(*e, towards(e))
        c.start()
        outs.append(c)
    self_out = pltpu.make_async_copy(send.at[mine_q], recv.at[mine_k], loc_sem.at[9])
    self_out.start()

    @pl.when(core == 1)
    def _():
        started = wz + first_copies(0) + first_copies(1) + first_copies(2)

        def go(c):
            c.start()
            started.append(c)

        sides = ((0, 1), (1, -1))

        def chain(step):
            for side, sign in sides:
                w = y_slice(0, mod(py - sign * step, NY))
                if step == 4:
                    w = w.at[half_rows[side]]
                if step > 0:
                    remote(w, w, gys.at[side, step - 1], gyr.at[side, step - 1],
                           at_y(sign)).wait_recv()
                if step == 3:
                    w = w.at[half_rows[side]]
                if step < 4:
                    go(remote(w, w, gys.at[side, step], gyr.at[side, step], at_y(sign)))

        half_rows = [slice(i * (GROWS * NX // 2), (i + 1) * (GROWS * NX // 2)) for i in range(2)]

        def x_part(m, xx, part):
            if m == 1:
                n = NY * GROWS
                return wu.at[ds(xx * n + part * (n // 2), n // 2), ALL]
            return wd.at[part * MID : (part + 1) * MID, ds(xx * QCOL, QCOL)]

        def from_y(m):
            for k in (1, 7, 2, 6, 3, 5, 4):
                w = y_slice(m, mod(py - k, NY))
                remote(w, w, uys.at[m - 1, k - 1], uyr.at[m - 1, k - 1], at_y(k)).wait_recv()

        def x_copy(m, side, sign, i, hops):
            w = x_part(m, mod(px - sign * hops, NX), side if i != 1 else 1 - side)
            return remote(w, w, uxs.at[m - 1, side, i], uxr.at[m - 1, side, i], at_x(sign))

        def along_x(m):
            for i in range(2):
                for side, sign in sides:
                    go(x_copy(m, side, sign, i, 0))

        def forward_x(m):
            for side, sign in sides:
                x_copy(m, side, sign, 0, 1).wait_recv()
                go(x_copy(m, side, sign, 2, 1))

        def from_x(m):
            for side, sign in sides:
                x_copy(m, side, sign, 1, 1).wait_recv()
                x_copy(m, side, sign, 2, 2).wait_recv()

        for k in (1, 3, 2):
            w = wg.at[ds(py * (NX * GROWS) + mod(px - k, NX) * GROWS, GROWS), ALL]
            remote(w, w, gxs.at[k - 1], gxr.at[k - 1], at_x(k)).wait_recv()
        chain(0)
        from_y(1)
        along_x(1)
        chain(1)
        from_y(2)
        along_x(2)
        forward_x(1)
        chain(2)
        forward_x(2)
        chain(3)
        from_x(1)
        chain(4)
        from_x(2)
        for c in started:
            c.wait_send()

    @pl.when(core == 0)
    def _():
        for c in wloads:
            c.wait()

    def gather_rows(first, count, pad, perm, dst):
        @pl.loop(0, 4)
        def _(n):
            cols = ds(n * 256, 256)
            rows = recv[first : first + count, :, cols].reshape(count * BLK, 256)
            dst[:, cols] = dot(perm[...], rows).astype(BF16)

        xl, xr = dst[0:pad, :], dst[pad : 2 * pad, :]
        dl, dr = dst[2 * pad : 3 * pad, :], dst[3 * pad :, :]
        a = dot(xl, wg[:HALF, :]) + dot(xr, wg[HALF:, :])
        b = dot(xl, wu[:HALF, :]) + dot(xr, wu[HALF:, :])
        dh = dot_nt(dl, wd[:, :HALF]) + dot_nt(dr, wd[:, HALF:])
        s = 1.0 / (1.0 + jnp.exp(-a))
        act = a * s
        hf = act * b
        da = (dh * b * s * (1.0 + a * (1.0 - s))).astype(BF16)
        db = (dh * act).astype(BF16)
        return hf, da, db

    def results(first, count, pad, perm_t, src, hf, da, db):
        h = hf.astype(BF16)
        for n in range(4):
            q, c0 = n // 2, QCOL * (n % 2)
            cols = slice(n * QCOL, (n + 1) * QCOL)
            src[q * pad : (q + 1) * pad, c0 : c0 + QCOL] = dot(h, wd[:, cols]).astype(BF16)
            grad = dot_nt(da, wg[cols, :]) + dot_nt(db, wu[cols, :])
            src[(2 + q) * pad : (3 + q) * pad, c0 : c0 + QCOL] = grad.astype(BF16)

        @pl.loop(0, 4)
        def _(n):
            cols = ds(n * 256, 256)
            rsend[first : first + count, :, cols] = (
                dot(perm_t[...], src[:, cols]).astype(BF16).reshape(count, BLK, 256)
            )

    for c in loads[2:]:
        c.wait()
    backs = []
    for e in exp_far:
        there(*e, whence(e)).wait_recv()
    hf_far, da, db = gather_rows(0, FAR, FPAD, pf, xf)
    results(0, FAR, FPAD, pft, yf, hf_far, da, db)
    self_out.wait()
    for e in exp_near:
        there(*e, whence(e)).wait_recv()
    for e in exp_far:
        c = back(*e, whence(e))
        c.start()
        backs.append(c)
    hf, da, db = gather_rows(FAR, NEAR, NPAD, pn, xn)

    htf = jnp.transpose(hf_far).astype(BF16)
    htn = jnp.transpose(hf).astype(BF16)
    for j in range(NX):
        q, c0 = 2 + j // 2, QCOL * (j % 2)
        piece = dot(htf, xf[q * FPAD : (q + 1) * FPAD, c0 : c0 + QCOL])
        piece = piece + dot(htn, xn[q * NPAD : (q + 1) * NPAD, c0 : c0 + QCOL])
        dw[j] = piece
        for g in range(2):
            dwb[g, j] = piece[:, g * GCOL : (g + 1) * GCOL].astype(BF16)
    right, left, across = mod(px + 1, NX), mod(px - 1, NX), mod(px + 2, NX)
    lo, hi = slice(0, MID), slice(MID, FFW)
    dx_copies = []
    for g in range(2):
        for i, (to, rr, side) in enumerate(
            ((across, lo, 1), (across, hi, -1), (right, hi, 1), (left, lo, -1))
        ):
            dst = (opp if i < 2 else pure).at[g, i % 2]
            c = remote(dwb.at[g, to, rr], dst, dxs.at[g, i], dxr.at[g, i], at_x(side))
            c.start()
            dx_copies.append(c)

    results(FAR, NEAR, NPAD, pnt, yn, hf, da, db)
    for e in exp_near[:4]:
        c = back(*e, whence(e))
        c.start()
        backs.append(c)
    self_back = pltpu.make_async_copy(rsend.at[mine_k], rrecv.at[mine_q], loc_sem.at[10])
    self_back.start()

    halves = [slice(g * GCOL, (g + 1) * GCOL) for g in range(2)]
    merged = []
    for g in range(2):
        for i, (to, rr, side) in enumerate(((right, lo, 1), (left, hi, -1))):
            dx_copies[4 * g + i].wait_recv()
            msend[g, i] = (dw[to, rr, halves[g]] + opp[g, i].astype(F32)).astype(BF16)
            c = remote(msend.at[g, i], mrecv.at[g, i], dxs.at[g, 4 + i], dxr.at[g, 4 + i],
                       at_x(side))
            c.start()
            merged.append(c)
    dy_copies = []
    for g in range(2):
        for c in dx_copies[4 * g + 2 : 4 * g + 4] + merged[2 * g : 2 * g + 2]:
            c.wait_recv()
        for i in range(NY):
            top = i < NY // 2
            rr = slice(i * DROWS, (i + 1) * DROWS)
            r0 = i * DROWS - (0 if top else MID)
            rm = slice(r0, r0 + DROWS)
            m, p = (0, 1) if top else (1, 0)
            got = mrecv[g, m, rm, :].astype(F32) + pure[g, p, rm, :].astype(F32)
            got = dw[px, rr, halves[g]] + got
            ysum[i, :, halves[g]] = got
            yb[g, i] = got.astype(BF16)
        for k in (4, 3, 5, 2, 6, 1, 7):
            c = remote(yb.at[g, mod(py + k, NY)], yrecv.at[g, k - 1], dys.at[g, k - 1],
                       dyr.at[g, k - 1], at_y(k))
            c.start()
            dy_copies.append(c)
    sums = []
    for g in range(2):
        for c in dy_copies[g * (NY - 1) : (g + 1) * (NY - 1)]:
            c.wait_recv()
        got = ysum[py, :, halves[g]]
        for k in range(NY - 1):
            got = got + yrecv[g, k].astype(F32)
        sums.append(got)
    part = jnp.concatenate(sums, axis=1)
    zsend[...] = part.astype(BF16)
    dz = remote(zsend, zrecv, dzs.at[0], dzr.at[0], at_z(8, other))

    @pl.when(core == 1)
    def _():
        dz.start()

    for e in exp_near[4:]:
        c = back(*e, whence(e))
        c.start()
        backs.append(c)

    def taking(b, first, count):
        rows = slice(first * BLK, (first + count) * BLK)
        return jnp.where(wantc[b : b + 1, rows] == tgt_c, 1.0, 0.0).astype(BF16)

    takes = [taking(b, 0, FAR) for b in range(4)]
    for e in src_far:
        back(*e, towards(e)).wait_recv()
    for n in range(4):
        cols = slice(n * 256, (n + 1) * 256)
        src = rrecv[0:FAR, :, cols].reshape(FROWS, 256)
        for b in range(4):
            oacc[b, :, cols] = dot(takes[b], src)

    @pl.when(core == 0)
    def _():
        dz.wait_recv()
        total = part + zrecv[...].astype(F32)
        for i in range(2 * NX):
            fsend[i, 0:6, :] = total[i * 6 : (i + 1) * 6, :]
            fsend[i, 6:8, :] = jnp.zeros((2, QCOL), F32)
        mine = pltpu.make_async_copy(fsend.at[2 * px], frecv.at[px], loc_sem.at[11])
        mine.start()
        fins = [remote(fsend.at[2 * px + 1], frecv.at[px], fs.at[0, 1], fr.at[px],
                       dev(py, px, 1, pz))]
        for k in range(1, NX):
            to = mod(px + k, NX)
            for c in range(2):
                fins.append(
                    remote(fsend.at[2 * to + c], frecv.at[px], fs.at[k, c], fr.at[px],
                           dev(py, to, c, pz))
                )
        for c in fins:
            c.start()
        mine.wait()
        for k in range(1, NX):
            src = mod(px + k, NX)
            remote(fsend.at[0], frecv.at[src], fs.at[k, 0], fr.at[src],
                   dev(py, src, 0, pz)).wait_recv()
        for c in fins:
            c.wait_send()

    @pl.when(core == 1)
    def _():
        for src in range(NX):
            remote(fsend.at[0], frecv.at[src], fs.at[0, 0], fr.at[src],
                   dev(py, src, 0, pz)).wait_recv()
        dz.wait_send()

    for j in range(NX):
        for i in range(6):
            dgrad_ref[i, :, j * QCOL : (j + 1) * QCOL] = frecv[j, i : i + 1, :]

    takes = [taking(b, FAR, NEAR) for b in range(4)]
    self_back.wait()
    for e in src_near:
        back(*e, towards(e)).wait_recv()
    gsum = jnp.zeros((TOK, 1), F32)
    for n in range(4):
        cols = slice(n * 256, (n + 1) * 256)
        src = rrecv[FAR:, :, cols].reshape(NROWS, 256)
        for q in range(2):
            full = slice(q * HALF + n * 256, q * HALF + (n + 1) * 256)
            o = oacc[q, :, cols] + dot(takes[q], src)
            out_ref[:, full] = (gw_c * o).astype(BF16)
            gsum = gsum + jnp.sum(cot[:, full].astype(F32) * o, axis=1, keepdims=True)
            tgrad_ref[:, full] = (oacc[2 + q, :, cols] + dot(takes[2 + q], src)).astype(BF16)
    ggrad_ref[...] = jnp.sum(jnp.where(eye, gsum, 0.0), axis=0, keepdims=True)

    for c in outs + backs + dx_copies + merged + dy_copies:
        c.wait_send()


def hand_over(*refs):
    n = len(refs) // 2
    for i in range(n):
        refs[n + i][...] = refs[i][...]


def gathering(count, pad):
    perm = np.zeros((4 * pad, count * BLK), np.float32)
    for r in range(count * BLK):
        k, w = divmod(r, BLK)
        half, w = divmod(w, 2 * CAP)
        kind, s = divmod(w, CAP)
        perm[(kind * 2 + half) * pad + k * CAP + s, r] = 1.0
    return jnp.asarray(perm, BF16), jnp.asarray(perm.T, BF16)


def wanted():
    want = np.full((8, NZ * BLK), -1, np.int32)
    for r in range(NZ * BLK):
        k, w = divmod(r, BLK)
        half, w = divmod(w, 2 * CAP)
        kind, s = divmod(w, CAP)
        want[kind * 2 + half, r] = k * CAP + s
    return jnp.asarray(want)


def shards(tokens, expert_ids, gate_weights, cotangent, gate_weight, up_weight, down_weight):
    hbm = pl.BlockSpec(memory_space=pl.ANY)
    vmem = pl.BlockSpec(memory_space=pltpu.VMEM)
    dma = pltpu.SemaphoreType.DMA
    mem = pltpu.VMEM
    outs = (
        jax.ShapeDtypeStruct((TOK, WIDTH), BF16),
        jax.ShapeDtypeStruct((TOK, WIDTH), BF16),
        jax.ShapeDtypeStruct((1, TOK), F32),
        jax.ShapeDtypeStruct((FFW // (2 * NX * NY), 1, WIDTH), F32),
    )
    results = pl.pallas_call(
        kernel,
        out_shape=outs,
        in_specs=[hbm, hbm, vmem, vmem] + [hbm] * 7 + [vmem],
        out_specs=(vmem,) * 4,
        scratch_shapes=[
            mem((TOK, WIDTH), BF16), mem((TOK, WIDTH), BF16), mem((4 * TOK, HALF), BF16),
            mem((WIDTH, FFW), BF16), mem((WIDTH, FFW), BF16), mem((FFW, WIDTH), BF16),
            mem((4 * FPAD, FROWS), BF16), mem((FROWS, 4 * FPAD), BF16),
            mem((4 * NPAD, NROWS), BF16), mem((NROWS, 4 * NPAD), BF16),
            mem((NZ, BLK, HALF), BF16), mem((NZ, BLK, HALF), BF16),
            mem((4 * FPAD, HALF), BF16), mem((4 * FPAD, HALF), BF16),
            mem((4 * NPAD, HALF), BF16), mem((4 * NPAD, HALF), BF16),
            mem((NZ, BLK, HALF), BF16), mem((NZ, BLK, HALF), BF16),
            mem((4, TOK, HALF), F32),
            mem((NX, FFW, QCOL), F32), mem((2, NX, FFW, GCOL), BF16),
            mem((2, 2, MID, GCOL), BF16), mem((2, 2, MID, GCOL), BF16),
            mem((2, 2, MID, GCOL), BF16), mem((2, 2, MID, GCOL), BF16),
            mem((NY, DROWS, QCOL), F32), mem((2, NY, DROWS, GCOL), BF16),
            mem((2, NY - 1, DROWS, GCOL), BF16),
            mem((DROWS, QCOL), BF16), mem((DROWS, QCOL), BF16),
            mem((2 * NX, 8, QCOL), F32), mem((NX, 8, QCOL), F32),
            dma((12,)),
            dma((NZ,)), dma((NZ,)), dma((NZ,)), dma((NZ,)),
            dma((3,)), dma((3,)), dma((3,)), dma((3,)),
            dma((2, 4)), dma((2, 4)), dma((2, NY - 1)), dma((2, NY - 1)),
            dma((2, 2, 3)), dma((2, 2, 3)),
            dma((2, 6)), dma((2, 6)), dma((2, NY - 1)), dma((2, NY - 1)),
            dma((1,)), dma((1,)), dma((NX, 2)), dma((NX,)), pltpu.SemaphoreType.REGULAR,
        ],
        compiler_params=pltpu.CompilerParams(
            collective_id=0, has_side_effects=True, vmem_limit_bytes=56 * 1024 * 1024
        ),
        cost_estimate=pl.CostEstimate(
            flops=6_000_000_000, bytes_accessed=16_000_000, transcendentals=100_000
        ),
    )(
        tokens, cotangent, expert_ids.reshape(1, TOK), gate_weights.reshape(1, TOK),
        gate_weight[0], up_weight[0], down_weight[0],
        *gathering(FAR, FPAD), *gathering(NEAR, NPAD), wanted(),
    )
    out, tgrad, ggrad, dgrad = pl.pallas_call(
        hand_over,
        out_shape=outs,
        in_specs=[vmem] * 4,
        out_specs=(vmem,) * 4,
        cost_estimate=pl.CostEstimate(flops=0, bytes_accessed=2_200_000, transcendentals=0),
    )(*results)
    return out, tgrad, ggrad.reshape(TOK, 1), jnp.transpose(dgrad, (1, 0, 2))


def solution(mesh):
    rows = P(("rep", "ep"), None)
    weight = P("ep", None, None)
    return jax.shard_map(
        shards,
        mesh=mesh,
        in_specs=(rows, rows, rows, rows, weight, weight, weight),
        out_specs=(rows, rows, rows, P("ep", "rep", None)),
        check_vma=False,
    )
```

```python
import jax
import jax.numpy as jnp
import numpy as np
from jax import lax
from jax.experimental import pallas as pl
from jax.experimental.pallas import tpu as pltpu
from jax.sharding import PartitionSpec as P

NX, NY, NZ = 4, 8, 16
TOK, WIDTH, FFW = 128, 2048, 384
CAP = 12
HALF = WIDTH // 2
BLK = 4 * CAP
FAR = 6
NEAR = NZ - FAR
FROWS, NROWS = FAR * BLK, NEAR * BLK
FPAD, NPAD = 80, 128
GROWS = WIDTH // (NX * NY)
DROWS = FFW // NY
QCOL = WIDTH // NX
MID = FFW // 2
GCOL = QCOL // 2
MESH = pl.DeviceIdType.MESH
F32 = jnp.float32
BF16 = jnp.bfloat16
NT = (((1,), (1,)), ((), ()))
ALL = slice(None)


def dot(a, b):
    return jnp.dot(a, b, preferred_element_type=F32)


def dot_nt(a, b):
    return lax.dot_general(a, b, NT, preferred_element_type=F32)


def ds(start, size):
    return pl.ds(pl.multiple_of(start, size), size)


def kernel(
    x_hbm, cot_hbm, ids_row, gw_row, wg_hbm, wu_hbm, wd_hbm, pf_hbm, pft_hbm, pn_hbm, pnt_hbm,
    wantc,
    out_ref, tgrad_ref, ggrad_ref, dgrad_ref,
    x, cot, z, wg, wu, wd, pf, pft, pn, pnt, send, recv, xf, yf, xn, yn, rsend, rrecv,
    oacc, dw, dwb, opp, pure, msend, mrecv, ysum, yb, yrecv, zsend, zrecv, fsend, frecv,
    loc_sem, s1, r1, s2, r2, wzs, wzr, gxs, gxr, gys, gyr, uys, uyr, uxs, uxr,
    dxs, dxr, dys, dyr, dzs, dzr, fs, fr, go_sem,
):
    rep = lax.axis_index("rep")
    pz = lax.axis_index("ep")
    core = lax.rem(rep, 2)
    px = lax.rem(rep // 2, NX)
    py = rep // (2 * NX)
    other = 1 - core

    def dev(y, x_, c, z_):
        return ((y * NX + x_) * 2 + c, z_)

    def mod(v, n):
        return lax.rem(v + n, n)

    def at_x(k):
        return dev(py, mod(px + k, NX), core, pz)

    def at_y(k):
        return dev(mod(py + k, NY), px, core, pz)

    def at_z(off, c):
        return dev(py, px, c, mod(pz + off, NZ))

    def remote(src, dst, ss, rs, target):
        return pltpu.make_async_remote_copy(
            src_ref=src, dst_ref=dst, send_sem=ss, recv_sem=rs,
            device_id=target, device_id_type=MESH,
        )

    tie, tie_other = 4 - 8 * core, 4 - 8 * other
    barrier = pltpu.get_barrier_semaphore()
    peers = [at_z(8, core), at_z(8, other), at_z(-4, core), at_z(4, core), at_z(tie, other)]
    for k in (4, 3, 5, 2, 6, 1, 7):
        peers.append(at_y(k))
    for o in (-3, 3, -2, 2, -1, 1):
        peers += [at_z(o, core), at_z(o, other)]
    for k in (2, 1, 3):
        peers.append(at_x(k))
        peers.append(dev(py, mod(px + k, NX), other, pz))
    peers.append(at_z(0, other))
    for peer in peers:
        pl.semaphore_signal(barrier, inc=1, device_id=peer, device_id_type=MESH)

    loads = [
        pltpu.make_async_copy(s, d, loc_sem.at[i])
        for i, (s, d) in enumerate(
            ((x_hbm, x), (cot_hbm, cot), (pf_hbm, pf), (pft_hbm, pft), (pn_hbm, pn), (pnt_hbm, pnt))
        )
    ]
    for c in loads:
        c.start()
    weights = (wg, wu, wd)
    wloads = [
        pltpu.make_async_copy(s, d, loc_sem.at[6 + i])
        for i, (s, d) in enumerate(zip((wg_hbm, wu_hbm, wd_hbm), weights))
    ]

    @pl.when(core == 0)
    def _():
        for c in wloads:
            c.start()

    def place_of(ids):
        u = lax.rem(ids - pz + (2 * NZ - 3), NZ)
        u = u + jnp.where((u >= 3) & (u < 8), 3, 0) - jnp.where((u >= 8) & (u < 11), 5, 0)
        return u

    lane = lax.broadcasted_iota(jnp.int32, (TOK, TOK), 1)
    sub = lax.broadcasted_iota(jnp.int32, (TOK, TOK), 0)
    eye = lane == sub
    q_r = place_of(ids_row[...])
    q_c = jnp.sum(jnp.where(eye, q_r, 0), axis=1, keepdims=True)
    gw_c = jnp.sum(jnp.where(eye, gw_row[...], 0.0), axis=1, keepdims=True)
    oh_r = (lax.broadcasted_iota(jnp.int32, (NZ, TOK), 0) == q_r).astype(F32)
    before = dot(oh_r.astype(BF16), (sub < lane).astype(F32).astype(BF16))
    slot_r = jnp.sum(before * oh_r, axis=0, keepdims=True).astype(jnp.int32)
    tgt_r = q_r * CAP + slot_r
    tgt_c = jnp.sum(jnp.where(eye, tgt_r, 0), axis=1, keepdims=True)

    def placing(first, count):
        ex = lax.broadcasted_iota(jnp.int32, (count, BLK, TOK), 0) + first
        row = lax.broadcasted_iota(jnp.int32, (count, BLK, TOK), 1)
        half = jnp.where(row >= 2 * CAP, 1, 0)
        row = row - 2 * CAP * half
        kind = jnp.where(row >= CAP, 1, 0)
        want = ex * CAP + row - CAP * kind
        quarter = jnp.where(want == tgt_r.reshape(1, 1, TOK), kind * 2 + half, -1)
        return jnp.concatenate(
            [
                jnp.where(quarter == b, 1.0, 0.0).reshape(count * BLK, TOK).astype(BF16)
                for b in range(4)
            ],
            axis=1,
        )

    place_far = placing(0, FAR)
    pl.semaphore_wait(barrier, len(peers))

    own = (
        (ds(py * (NX * GROWS) + px * GROWS, GROWS), ALL),
        (ds(px * (NY * GROWS) + py * GROWS, GROWS), ALL),
        (ds(py * DROWS, DROWS), ds(px * QCOL, QCOL)),
    )
    wz = [
        remote(h.at[i], w.at[i], wzs.at[m], wzr.at[m], at_z(8, core))
        for m, (h, w, i) in enumerate(zip((wg_hbm, wu_hbm, wd_hbm), weights, own))
    ]

    @pl.when(core == 1)
    def _():
        for m in (1, 2, 0):
            wz[m].start()

    for c in loads[:2]:
        c.wait()
    z[0:TOK, :] = x[:, :HALF]
    z[TOK : 2 * TOK, :] = x[:, HALF:]
    dout = (gw_c * cot[...].astype(F32)).astype(BF16)
    z[2 * TOK : 3 * TOK, :] = dout[:, :HALF]
    z[3 * TOK :, :] = dout[:, HALF:]

    def build(place, first, count):
        @pl.loop(0, 4)
        def _(n):
            cols = ds(n * 256, 256)
            send[first : first + count, :, cols] = (
                dot(place, z[:, cols]).astype(BF16).reshape(count, BLK, 256)
            )

    build(place_far, 0, FAR)

    def as_source():
        far = [(tie, core, 1, 4 + core), (tie, other, 4, 4 + core)]
        for c in (core, other):
            far += [(3, c, 3 * c, 2 + core), (-3, c, 5 - 3 * c, core)]
        near = []
        for o in (2, -2, 1, -1):
            for c in (core, other):
                near.append((o, c, 13 + o - 5 * c, 10 + 2 * o + core))
        near.append((0, other, 13 - 5 * other, 10 + core))
        return far, near

    def as_expert():
        far = [(tie, core, 1, 4 + core), (tie_other, other, 4, 4 + other)]
        for c in (core, other):
            far += [(3, c, 3 * core, 2 + c), (-3, c, 5 - 3 * core, c)]
        near = []
        for o in (2, -2, 1, -1):
            for c in (core, other):
                near.append((o, c, 13 + o - 5 * core, 10 + 2 * o + c))
        near.append((0, other, 13 - 5 * core, 10 + other))
        return far, near

    def there(off, c, q, k, target):
        return remote(send.at[q], recv.at[k], s1.at[q], r1.at[k], target)

    def back(off, c, q, k, target):
        return remote(rsend.at[k], rrecv.at[q], s2.at[k], r2.at[q], target)

    def towards(e):
        return at_z(e[0], e[1])

    def whence(e):
        return at_z(-e[0], e[1])

    mine_q, mine_k = 13 - 5 * core, 10 + core
    src_far, src_near = as_source()
    exp_far, exp_near = as_expert()

    outs = [there(*e, towards(e)) for e in src_far]
    for c in outs:
        c.start()
    build(placing(FAR, NEAR), FAR, NEAR)

    def y_slice(m, y):
        if m == 0:
            return wg.at[ds(y * (NX * GROWS), NX * GROWS), ALL]
        if m == 1:
            return wu.at[ds(px * (NY * GROWS) + y * GROWS, GROWS), ALL]
        return wd.at[ds(y * DROWS, DROWS), ds(px * QCOL, QCOL)]

    def first_copies(m):
        if m == 0:
            w = wg.at[own[0]]
            return [remote(w, w, gxs.at[k - 1], gxr.at[k - 1], at_x(k)) for k in (2, 1, 3)]
        w = y_slice(m, py)
        return [
            remote(w, w, uys.at[m - 1, k - 1], uyr.at[m - 1, k - 1], at_y(k))
            for k in (4, 3, 5, 2, 6, 1, 7)
        ]

    @pl.when(core == 1)
    def _():
        for m in (1, 2, 0):
            wz[m].wait_recv()
            for c in first_copies(m):
                c.start()
        pl.semaphore_signal(go_sem, inc=1, device_id=at_z(0, other), device_id_type=MESH)

    @pl.when(core == 0)
    def _():
        pl.semaphore_wait(go_sem, 1)

    for e in src_near:
        c = there(*e, towards(e))
        c.start()
        outs.append(c)
    self_out = pltpu.make_async_copy(send.at[mine_q], recv.at[mine_k], loc_sem.at[9])
    self_out.start()

    @pl.when(core == 1)
    def _():
        started = wz + first_copies(0) + first_copies(1) + first_copies(2)

        def go(c):
            c.start()
            started.append(c)

        sides = ((0, 1), (1, -1))

        def chain(step):
            for side, sign in sides:
                w = y_slice(0, mod(py - sign * step, NY))
                if step == 4:
                    w = w.at[half_rows[side]]
                if step > 0:
                    remote(w, w, gys.at[side, step - 1], gyr.at[side, step - 1],
                           at_y(sign)).wait_recv()
                if step == 3:
                    w = w.at[half_rows[side]]
                if step < 4:
                    go(remote(w, w, gys.at[side, step], gyr.at[side, step], at_y(sign)))

        half_rows = [slice(i * (GROWS * NX // 2), (i + 1) * (GROWS * NX // 2)) for i in range(2)]

        def x_part(m, xx, part):
            if m == 1:
                n = NY * GROWS
                return wu.at[ds(xx * n + part * (n // 2), n // 2), ALL]
            return wd.at[part * MID : (part + 1) * MID, ds(xx * QCOL, QCOL)]

        def from_y(m):
            for k in (1, 7, 2, 6, 3, 5, 4):
                w = y_slice(m, mod(py - k, NY))
                remote(w, w, uys.at[m - 1, k - 1], uyr.at[m - 1, k - 1], at_y(k)).wait_recv()

        def x_copy(m, side, sign, i, hops):
            w = x_part(m, mod(px - sign * hops, NX), side if i != 1 else 1 - side)
            return remote(w, w, uxs.at[m - 1, side, i], uxr.at[m - 1, side, i], at_x(sign))

        def along_x(m):
            for i in range(2):
                for side, sign in sides:
                    go(x_copy(m, side, sign, i, 0))

        def forward_x(m):
            for side, sign in sides:
                x_copy(m, side, sign, 0, 1).wait_recv()
                go(x_copy(m, side, sign, 2, 1))

        def from_x(m):
            for side, sign in sides:
                x_copy(m, side, sign, 1, 1).wait_recv()
                x_copy(m, side, sign, 2, 2).wait_recv()

        for k in (1, 3, 2):
            w = wg.at[ds(py * (NX * GROWS) + mod(px - k, NX) * GROWS, GROWS), ALL]
            remote(w, w, gxs.at[k - 1], gxr.at[k - 1], at_x(k)).wait_recv()
        chain(0)
        from_y(1)
        along_x(1)
        chain(1)
        from_y(2)
        along_x(2)
        forward_x(1)
        chain(2)
        forward_x(2)
        chain(3)
        from_x(1)
        chain(4)
        from_x(2)
        for c in started:
            c.wait_send()

    @pl.when(core == 0)
    def _():
        for c in wloads:
            c.wait()

    def gather_rows(first, count, pad, perm, dst):
        @pl.loop(0, 4)
        def _(n):
            cols = ds(n * 256, 256)
            rows = recv[first : first + count, :, cols].reshape(count * BLK, 256)
            dst[:, cols] = dot(perm[...], rows).astype(BF16)

        xl, xr = dst[0:pad, :], dst[pad : 2 * pad, :]
        dl, dr = dst[2 * pad : 3 * pad, :], dst[3 * pad :, :]
        a = dot(xl, wg[:HALF, :]) + dot(xr, wg[HALF:, :])
        b = dot(xl, wu[:HALF, :]) + dot(xr, wu[HALF:, :])
        dh = dot_nt(dl, wd[:, :HALF]) + dot_nt(dr, wd[:, HALF:])
        s = 1.0 / (1.0 + jnp.exp(-a))
        act = a * s
        hf = act * b
        da = (dh * b * s * (1.0 + a * (1.0 - s))).astype(BF16)
        db = (dh * act).astype(BF16)
        return hf, da, db

    def results(first, count, pad, perm_t, src, hf, da, db):
        h = hf.astype(BF16)
        for n in range(4):
            q, c0 = n // 2, QCOL * (n % 2)
            cols = slice(n * QCOL, (n + 1) * QCOL)
            src[q * pad : (q + 1) * pad, c0 : c0 + QCOL] = dot(h, wd[:, cols]).astype(BF16)
            grad = dot_nt(da, wg[cols, :]) + dot_nt(db, wu[cols, :])
            src[(2 + q) * pad : (3 + q) * pad, c0 : c0 + QCOL] = grad.astype(BF16)

        @pl.loop(0, 4)
        def _(n):
            cols = ds(n * 256, 256)
            rsend[first : first + count, :, cols] = (
                dot(perm_t[...], src[:, cols]).astype(BF16).reshape(count, BLK, 256)
            )

    for c in loads[2:]:
        c.wait()
    backs = []
    for e in exp_far:
        there(*e, whence(e)).wait_recv()
    hf_far, da_far, db_far = gather_rows(0, FAR, FPAD, pf, xf)

    @pl.when(core == 0)
    def _():
        results(0, FAR, FPAD, pft, yf, hf_far, da_far, db_far)

    self_out.wait()
    for e in exp_near:
        there(*e, whence(e)).wait_recv()

    @pl.when(core == 0)
    def _():
        for e in exp_far:
            back(*e, whence(e)).start()

    hf, da, db = gather_rows(FAR, NEAR, NPAD, pn, xn)

    htf = jnp.transpose(hf_far).astype(BF16)
    htn = jnp.transpose(hf).astype(BF16)
    for j in range(NX):
        q, c0 = 2 + j // 2, QCOL * (j % 2)
        piece = dot(htf, xf[q * FPAD : (q + 1) * FPAD, c0 : c0 + QCOL])
        piece = piece + dot(htn, xn[q * NPAD : (q + 1) * NPAD, c0 : c0 + QCOL])
        dw[j] = piece
        for g in range(2):
            dwb[g, j] = piece[:, g * GCOL : (g + 1) * GCOL].astype(BF16)
    right, left, across = mod(px + 1, NX), mod(px - 1, NX), mod(px + 2, NX)
    lo, hi = slice(0, MID), slice(MID, FFW)
    dx_copies = []
    for g in range(2):
        for i, (to, rr, side) in enumerate(
            ((across, lo, 1), (across, hi, -1), (right, hi, 1), (left, lo, -1))
        ):
            dst = (opp if i < 2 else pure).at[g, i % 2]
            c = remote(dwb.at[g, to, rr], dst, dxs.at[g, i], dxr.at[g, i], at_x(side))
            c.start()
            dx_copies.append(c)

    @pl.when(core == 1)
    def _():
        results(0, FAR, FPAD, pft, yf, hf_far, da_far, db_far)
        for e in exp_far:
            back(*e, whence(e)).start()

    backs += [back(*e, whence(e)) for e in exp_far]
    results(FAR, NEAR, NPAD, pnt, yn, hf, da, db)
    for e in exp_near[0:3:2]:
        c = back(*e, whence(e))
        c.start()
        backs.append(c)
    self_back = pltpu.make_async_copy(rsend.at[mine_k], rrecv.at[mine_q], loc_sem.at[10])
    self_back.start()

    halves = [slice(g * GCOL, (g + 1) * GCOL) for g in range(2)]
    merged = []
    for g in range(2):
        for i, (to, rr, side) in enumerate(((right, lo, 1), (left, hi, -1))):
            dx_copies[4 * g + i].wait_recv()
            msend[g, i] = (dw[to, rr, halves[g]] + opp[g, i].astype(F32)).astype(BF16)
            c = remote(msend.at[g, i], mrecv.at[g, i], dxs.at[g, 4 + i], dxr.at[g, 4 + i],
                       at_x(side))
            c.start()
            merged.append(c)
    dy_copies = []
    for g in range(2):
        for c in dx_copies[4 * g + 2 : 4 * g + 4] + merged[2 * g : 2 * g + 2]:
            c.wait_recv()
        for i in range(NY):
            top = i < NY // 2
            rr = slice(i * DROWS, (i + 1) * DROWS)
            r0 = i * DROWS - (0 if top else MID)
            rm = slice(r0, r0 + DROWS)
            m, p = (0, 1) if top else (1, 0)
            got = mrecv[g, m, rm, :].astype(F32) + pure[g, p, rm, :].astype(F32)
            got = dw[px, rr, halves[g]] + got
            ysum[i, :, halves[g]] = got
            yb[g, i] = got.astype(BF16)
        for k in (4, 3, 5, 2, 6, 1, 7):
            c = remote(yb.at[g, mod(py + k, NY)], yrecv.at[g, k - 1], dys.at[g, k - 1],
                       dyr.at[g, k - 1], at_y(k))
            c.start()
            dy_copies.append(c)
    sums, dz = [], []
    for g in range(2):
        for c in dy_copies[g * (NY - 1) : (g + 1) * (NY - 1)]:
            c.wait_recv()
        got = ysum[py, :, halves[g]]
        for k in range(NY - 1):
            got = got + yrecv[g, k].astype(F32)
        sums.append(got)
        zsend[g] = got.astype(BF16)
        c = remote(zsend.at[g], zrecv.at[g], dzs.at[g], dzr.at[g], at_z(8, other))
        dz.append(c)

        @pl.when(core == 1)
        def _():
            c.start()

    for e in exp_near[1:4:2] + exp_near[4:]:
        c = back(*e, whence(e))
        c.start()
        backs.append(c)

    def taking(b, first, count):
        rows = slice(first * BLK, (first + count) * BLK)
        return jnp.where(wantc[b : b + 1, rows] == tgt_c, 1.0, 0.0).astype(BF16)

    takes = [taking(b, 0, FAR) for b in range(4)]
    for e in src_far:
        back(*e, towards(e)).wait_recv()
    for n in range(4):
        cols = slice(n * 256, (n + 1) * 256)
        src = rrecv[0:FAR, :, cols].reshape(FROWS, 256)
        for b in range(4):
            oacc[b, :, cols] = dot(takes[b], src)

    def fin_copies():
        fins = [remote(fsend.at[2 * px + 1], frecv.at[px], fs.at[0, 1], fr.at[px],
                       dev(py, px, 1, pz))]
        for k in range(1, NX):
            to = mod(px + k, NX)
            for c in range(2):
                fins.append(
                    remote(fsend.at[2 * to + c], frecv.at[px], fs.at[k, c], fr.at[px],
                           dev(py, to, c, pz))
                )
        return fins

    mine = pltpu.make_async_copy(fsend.at[2 * px], frecv.at[px], loc_sem.at[11])

    @pl.when(core == 0)
    def _():
        total = []
        for g in range(2):
            dz[g].wait_recv()
            total.append(sums[g] + zrecv[g].astype(F32))
        total = jnp.concatenate(total, axis=1)
        for i in range(2 * NX):
            fsend[i, 0:6, :] = total[i * 6 : (i + 1) * 6, :]
            fsend[i, 6:8, :] = jnp.zeros((2, QCOL), F32)
        mine.start()
        for c in fin_copies():
            c.start()

    takes = [taking(b, FAR, NEAR) for b in range(4)]
    self_back.wait()
    for e in src_near:
        back(*e, towards(e)).wait_recv()
    gsum = jnp.zeros((TOK, 1), F32)
    for n in range(4):
        cols = slice(n * 256, (n + 1) * 256)
        src = rrecv[FAR:, :, cols].reshape(NROWS, 256)
        for q in range(2):
            full = slice(q * HALF + n * 256, q * HALF + (n + 1) * 256)
            o = oacc[q, :, cols] + dot(takes[q], src)
            out_ref[:, full] = (gw_c * o).astype(BF16)
            gsum = gsum + jnp.sum(cot[:, full].astype(F32) * o, axis=1, keepdims=True)
            tgrad_ref[:, full] = (oacc[2 + q, :, cols] + dot(takes[2 + q], src)).astype(BF16)
    ggrad_ref[...] = jnp.sum(jnp.where(eye, gsum, 0.0), axis=0, keepdims=True)

    @pl.when(core == 0)
    def _():
        mine.wait()
        for k in range(1, NX):
            src = mod(px + k, NX)
            remote(fsend.at[0], frecv.at[src], fs.at[k, 0], fr.at[src],
                   dev(py, src, 0, pz)).wait_recv()
        for c in fin_copies():
            c.wait_send()

    @pl.when(core == 1)
    def _():
        for src in range(NX):
            remote(fsend.at[0], frecv.at[src], fs.at[0, 0], fr.at[src],
                   dev(py, src, 0, pz)).wait_recv()
        for c in dz:
            c.wait_send()

    for j in range(NX):
        for i in range(6):
            dgrad_ref[i, :, j * QCOL : (j + 1) * QCOL] = frecv[j, i : i + 1, :]

    for c in outs + backs + dx_copies + merged + dy_copies:
        c.wait_send()


def hand_over(*refs):
    n = len(refs) // 2
    for i in range(n):
        refs[n + i][...] = refs[i][...]


def gathering(count, pad):
    perm = np.zeros((4 * pad, count * BLK), np.float32)
    for r in range(count * BLK):
        k, w = divmod(r, BLK)
        half, w = divmod(w, 2 * CAP)
        kind, s = divmod(w, CAP)
        perm[(kind * 2 + half) * pad + k * CAP + s, r] = 1.0
    return jnp.asarray(perm, BF16), jnp.asarray(perm.T, BF16)


def wanted():
    want = np.full((8, NZ * BLK), -1, np.int32)
    for r in range(NZ * BLK):
        k, w = divmod(r, BLK)
        half, w = divmod(w, 2 * CAP)
        kind, s = divmod(w, CAP)
        want[kind * 2 + half, r] = k * CAP + s
    return jnp.asarray(want)


def shards(tokens, expert_ids, gate_weights, cotangent, gate_weight, up_weight, down_weight):
    hbm = pl.BlockSpec(memory_space=pl.ANY)
    vmem = pl.BlockSpec(memory_space=pltpu.VMEM)
    dma = pltpu.SemaphoreType.DMA
    mem = pltpu.VMEM
    outs = (
        jax.ShapeDtypeStruct((TOK, WIDTH), BF16),
        jax.ShapeDtypeStruct((TOK, WIDTH), BF16),
        jax.ShapeDtypeStruct((1, TOK), F32),
        jax.ShapeDtypeStruct((FFW // (2 * NX * NY), 1, WIDTH), F32),
    )
    results = pl.pallas_call(
        kernel,
        out_shape=outs,
        in_specs=[hbm, hbm, vmem, vmem] + [hbm] * 7 + [vmem],
        out_specs=(vmem,) * 4,
        scratch_shapes=[
            mem((TOK, WIDTH), BF16), mem((TOK, WIDTH), BF16), mem((4 * TOK, HALF), BF16),
            mem((WIDTH, FFW), BF16), mem((WIDTH, FFW), BF16), mem((FFW, WIDTH), BF16),
            mem((4 * FPAD, FROWS), BF16), mem((FROWS, 4 * FPAD), BF16),
            mem((4 * NPAD, NROWS), BF16), mem((NROWS, 4 * NPAD), BF16),
            mem((NZ, BLK, HALF), BF16), mem((NZ, BLK, HALF), BF16),
            mem((4 * FPAD, HALF), BF16), mem((4 * FPAD, HALF), BF16),
            mem((4 * NPAD, HALF), BF16), mem((4 * NPAD, HALF), BF16),
            mem((NZ, BLK, HALF), BF16), mem((NZ, BLK, HALF), BF16),
            mem((4, TOK, HALF), F32),
            mem((NX, FFW, QCOL), F32), mem((2, NX, FFW, GCOL), BF16),
            mem((2, 2, MID, GCOL), BF16), mem((2, 2, MID, GCOL), BF16),
            mem((2, 2, MID, GCOL), BF16), mem((2, 2, MID, GCOL), BF16),
            mem((NY, DROWS, QCOL), F32), mem((2, NY, DROWS, GCOL), BF16),
            mem((2, NY - 1, DROWS, GCOL), BF16),
            mem((2, DROWS, GCOL), BF16), mem((2, DROWS, GCOL), BF16),
            mem((2 * NX, 8, QCOL), F32), mem((NX, 8, QCOL), F32),
            dma((12,)),
            dma((NZ,)), dma((NZ,)), dma((NZ,)), dma((NZ,)),
            dma((3,)), dma((3,)), dma((3,)), dma((3,)),
            dma((2, 4)), dma((2, 4)), dma((2, NY - 1)), dma((2, NY - 1)),
            dma((2, 2, 3)), dma((2, 2, 3)),
            dma((2, 6)), dma((2, 6)), dma((2, NY - 1)), dma((2, NY - 1)),
            dma((2,)), dma((2,)), dma((NX, 2)), dma((NX,)), pltpu.SemaphoreType.REGULAR,
        ],
        compiler_params=pltpu.CompilerParams(
            collective_id=0, has_side_effects=True, vmem_limit_bytes=56 * 1024 * 1024
        ),
        cost_estimate=pl.CostEstimate(
            flops=6_000_000_000, bytes_accessed=16_000_000, transcendentals=100_000
        ),
    )(
        tokens, cotangent, expert_ids.reshape(1, TOK), gate_weights.reshape(1, TOK),
        gate_weight[0], up_weight[0], down_weight[0],
        *gathering(FAR, FPAD), *gathering(NEAR, NPAD), wanted(),
    )
    out, tgrad, ggrad, dgrad = pl.pallas_call(
        hand_over,
        out_shape=outs,
        in_specs=[vmem] * 4,
        out_specs=(vmem,) * 4,
        cost_estimate=pl.CostEstimate(flops=0, bytes_accessed=2_200_000, transcendentals=0),
    )(*results)
    return out, tgrad, ggrad.reshape(TOK, 1), jnp.transpose(dgrad, (1, 0, 2))


def solution(mesh):
    rows = P(("rep", "ep"), None)
    weight = P("ep", None, None)
    return jax.shard_map(
        shards,
        mesh=mesh,
        in_specs=(rows, rows, rows, rows, weight, weight, weight),
        out_specs=(rows, rows, rows, P("ep", "rep", None)),
        check_vma=False,
    )
```

```python
import jax
import jax.numpy as jnp
import numpy as np
from jax import lax
from jax.experimental import pallas as pl
from jax.experimental.pallas import tpu as pltpu
from jax.sharding import PartitionSpec as P

NX, NY, NZ = 4, 8, 16
TOK, WIDTH, FFW = 128, 2048, 384
CAP = 12
HALF = WIDTH // 2
BLK = 4 * CAP
FAR = 6
NEAR = NZ - FAR
FROWS, NROWS = FAR * BLK, NEAR * BLK
FPAD, NPAD = 80, 128
GROWS = WIDTH // (NX * NY)
DROWS = FFW // NY
QCOL = WIDTH // NX
MID = FFW // 2
GCOL = QCOL // 2
MESH = pl.DeviceIdType.MESH
F32 = jnp.float32
BF16 = jnp.bfloat16
NT = (((1,), (1,)), ((), ()))
ALL = slice(None)


def dot(a, b):
    return jnp.dot(a, b, preferred_element_type=F32)


def dot_nt(a, b):
    return lax.dot_general(a, b, NT, preferred_element_type=F32)


def ds(start, size):
    return pl.ds(pl.multiple_of(start, size), size)


def kernel(
    x_hbm, cot_hbm, ids_row, gw_row, wg_hbm, wu_hbm, wd_hbm, pf_hbm, pft_hbm, pn_hbm, pnt_hbm,
    wantc,
    out_hbm, tgrad_hbm, ggrad_hbm, dgrad_hbm,
    x, cot, z, wg, wu, wd, pf, pft, pn, pnt, send, recv, xf, yf, xn, yn, rsend, rrecv,
    oacc, dw, dwb, opp, pure, msend, mrecv, ysum, yb, yrecv, zsend, zrecv, fsend, frecv,
    loc_sem, s1, r1, s2, r2, wzs, wzr, gxs, gxr, gys, gyr, uys, uyr, uxs, uxr,
    dxs, dxr, dys, dyr, dzs, dzr, fs, fr, go_sem, out_ref, tgrad_ref, ggrad_ref, dgrad_ref,
    res_sem,
):
    rep = lax.axis_index("rep")
    pz = lax.axis_index("ep")
    core = lax.rem(rep, 2)
    px = lax.rem(rep // 2, NX)
    py = rep // (2 * NX)
    other = 1 - core

    def dev(y, x_, c, z_):
        return ((y * NX + x_) * 2 + c, z_)

    def mod(v, n):
        return lax.rem(v + n, n)

    def at_x(k):
        return dev(py, mod(px + k, NX), core, pz)

    def at_y(k):
        return dev(mod(py + k, NY), px, core, pz)

    def at_z(off, c):
        return dev(py, px, c, mod(pz + off, NZ))

    def remote(src, dst, ss, rs, target):
        return pltpu.make_async_remote_copy(
            src_ref=src, dst_ref=dst, send_sem=ss, recv_sem=rs,
            device_id=target, device_id_type=MESH,
        )

    tie, tie_other = 4 - 8 * core, 4 - 8 * other
    barrier = pltpu.get_barrier_semaphore()
    peers = [at_z(8, core), at_z(8, other), at_z(-4, core), at_z(4, core), at_z(tie, other)]
    for k in (4, 3, 5, 2, 6, 1, 7):
        peers.append(at_y(k))
    for o in (-3, 3, -2, 2, -1, 1):
        peers += [at_z(o, core), at_z(o, other)]
    for k in (2, 1, 3):
        peers.append(at_x(k))
        peers.append(dev(py, mod(px + k, NX), other, pz))
    peers.append(at_z(0, other))
    for peer in peers:
        pl.semaphore_signal(barrier, inc=1, device_id=peer, device_id_type=MESH)

    loads = [
        pltpu.make_async_copy(s, d, loc_sem.at[i])
        for i, (s, d) in enumerate(
            ((x_hbm, x), (cot_hbm, cot), (pf_hbm, pf), (pft_hbm, pft), (pn_hbm, pn), (pnt_hbm, pnt))
        )
    ]
    for c in loads:
        c.start()
    weights = (wg, wu, wd)
    wloads = [
        pltpu.make_async_copy(s, d, loc_sem.at[6 + i])
        for i, (s, d) in enumerate(zip((wg_hbm, wu_hbm, wd_hbm), weights))
    ]

    @pl.when(core == 0)
    def _():
        for c in wloads:
            c.start()

    def place_of(ids):
        u = lax.rem(ids - pz + (2 * NZ - 3), NZ)
        u = u + jnp.where((u >= 3) & (u < 8), 3, 0) - jnp.where((u >= 8) & (u < 11), 5, 0)
        return u

    lane = lax.broadcasted_iota(jnp.int32, (TOK, TOK), 1)
    sub = lax.broadcasted_iota(jnp.int32, (TOK, TOK), 0)
    eye = lane == sub
    q_r = place_of(ids_row[...])
    q_c = jnp.sum(jnp.where(eye, q_r, 0), axis=1, keepdims=True)
    gw_c = jnp.sum(jnp.where(eye, gw_row[...], 0.0), axis=1, keepdims=True)
    oh_r = (lax.broadcasted_iota(jnp.int32, (NZ, TOK), 0) == q_r).astype(F32)
    before = dot(oh_r.astype(BF16), (sub < lane).astype(F32).astype(BF16))
    slot_r = jnp.sum(before * oh_r, axis=0, keepdims=True).astype(jnp.int32)
    tgt_r = q_r * CAP + slot_r
    tgt_c = jnp.sum(jnp.where(eye, tgt_r, 0), axis=1, keepdims=True)

    def placing(first, count):
        ex = lax.broadcasted_iota(jnp.int32, (count, BLK, TOK), 0) + first
        row = lax.broadcasted_iota(jnp.int32, (count, BLK, TOK), 1)
        half = jnp.where(row >= 2 * CAP, 1, 0)
        row = row - 2 * CAP * half
        kind = jnp.where(row >= CAP, 1, 0)
        want = ex * CAP + row - CAP * kind
        quarter = jnp.where(want == tgt_r.reshape(1, 1, TOK), kind * 2 + half, -1)
        return jnp.concatenate(
            [
                jnp.where(quarter == b, 1.0, 0.0).reshape(count * BLK, TOK).astype(BF16)
                for b in range(4)
            ],
            axis=1,
        )

    place_far = placing(0, FAR)
    for c in loads[:2]:
        c.wait()
    z[0:TOK, :] = x[:, :HALF]
    z[TOK : 2 * TOK, :] = x[:, HALF:]
    dout = (gw_c * cot[...].astype(F32)).astype(BF16)
    z[2 * TOK : 3 * TOK, :] = dout[:, :HALF]
    z[3 * TOK :, :] = dout[:, HALF:]

    def build(place, first, count):
        @pl.loop(0, 4)
        def _(n):
            cols = ds(n * 256, 256)
            send[first : first + count, :, cols] = (
                dot(place, z[:, cols]).astype(BF16).reshape(count, BLK, 256)
            )

    build(place_far, 0, FAR)
    pl.semaphore_wait(barrier, len(peers))

    own = (
        (ds(py * (NX * GROWS) + px * GROWS, GROWS), ALL),
        (ds(px * (NY * GROWS) + py * GROWS, GROWS), ALL),
        (ds(py * DROWS, DROWS), ds(px * QCOL, QCOL)),
    )
    wz = [
        remote(h.at[i], w.at[i], wzs.at[m], wzr.at[m], at_z(8, core))
        for m, (h, w, i) in enumerate(zip((wg_hbm, wu_hbm, wd_hbm), weights, own))
    ]

    @pl.when(core == 1)
    def _():
        for m in (1, 2, 0):
            wz[m].start()

    def as_source():
        far = [(tie, core, 1, 4 + core), (tie, other, 4, 4 + core)]
        for c in (core, other):
            far += [(3, c, 3 * c, 2 + core), (-3, c, 5 - 3 * c, core)]
        near = []
        for o in (2, -2, 1, -1):
            for c in (core, other):
                near.append((o, c, 13 + o - 5 * c, 10 + 2 * o + core))
        near.append((0, other, 13 - 5 * other, 10 + core))
        return far, near

    def as_expert():
        far = [(tie, core, 1, 4 + core), (tie_other, other, 4, 4 + other)]
        for c in (core, other):
            far += [(3, c, 3 * core, 2 + c), (-3, c, 5 - 3 * core, c)]
        near = []
        for o in (2, -2, 1, -1):
            for c in (core, other):
                near.append((o, c, 13 + o - 5 * core, 10 + 2 * o + c))
        near.append((0, other, 13 - 5 * core, 10 + other))
        return far, near

    def there(off, c, q, k, target):
        return remote(send.at[q], recv.at[k], s1.at[q], r1.at[k], target)

    def back(off, c, q, k, target):
        return remote(rsend.at[k], rrecv.at[q], s2.at[k], r2.at[q], target)

    def towards(e):
        return at_z(e[0], e[1])

    def whence(e):
        return at_z(-e[0], e[1])

    mine_q, mine_k = 13 - 5 * core, 10 + core
    src_far, src_near = as_source()
    exp_far, exp_near = as_expert()

    outs = [there(*e, towards(e)) for e in src_far]
    for c in outs:
        c.start()
    build(placing(FAR, NEAR), FAR, NEAR)

    def y_slice(m, y):
        if m == 0:
            return wg.at[ds(y * (NX * GROWS), NX * GROWS), ALL]
        if m == 1:
            return wu.at[ds(px * (NY * GROWS) + y * GROWS, GROWS), ALL]
        return wd.at[ds(y * DROWS, DROWS), ds(px * QCOL, QCOL)]

    def first_copies(m):
        if m == 0:
            w = wg.at[own[0]]
            return [remote(w, w, gxs.at[k - 1], gxr.at[k - 1], at_x(k)) for k in (2, 1, 3)]
        w = y_slice(m, py)
        return [
            remote(w, w, uys.at[m - 1, k - 1], uyr.at[m - 1, k - 1], at_y(k))
            for k in (4, 3, 5, 2, 6, 1, 7)
        ]

    @pl.when(core == 1)
    def _():
        for m in (1, 2, 0):
            wz[m].wait_recv()
            for c in first_copies(m):
                c.start()
        pl.semaphore_signal(go_sem, inc=1, device_id=at_z(0, other), device_id_type=MESH)

    @pl.when(core == 0)
    def _():
        pl.semaphore_wait(go_sem, 1)

    for e in src_near:
        c = there(*e, towards(e))
        c.start()
        outs.append(c)
    self_out = pltpu.make_async_copy(send.at[mine_q], recv.at[mine_k], loc_sem.at[9])
    self_out.start()

    @pl.when(core == 1)
    def _():
        started = wz + first_copies(0) + first_copies(1) + first_copies(2)

        def go(c):
            c.start()
            started.append(c)

        sides = ((0, 1), (1, -1))

        def chain(step):
            for side, sign in sides:
                w = y_slice(0, mod(py - sign * step, NY))
                if step == 4:
                    w = w.at[half_rows[side]]
                if step > 0:
                    remote(w, w, gys.at[side, step - 1], gyr.at[side, step - 1],
                           at_y(sign)).wait_recv()
                if step == 3:
                    w = w.at[half_rows[side]]
                if step < 4:
                    go(remote(w, w, gys.at[side, step], gyr.at[side, step], at_y(sign)))

        half_rows = [slice(i * (GROWS * NX // 2), (i + 1) * (GROWS * NX // 2)) for i in range(2)]

        def x_part(m, xx, part):
            if m == 1:
                n = NY * GROWS
                return wu.at[ds(xx * n + part * (n // 2), n // 2), ALL]
            return wd.at[part * MID : (part + 1) * MID, ds(xx * QCOL, QCOL)]

        def from_y(m):
            for k in (1, 7, 2, 6, 3, 5, 4):
                w = y_slice(m, mod(py - k, NY))
                remote(w, w, uys.at[m - 1, k - 1], uyr.at[m - 1, k - 1], at_y(k)).wait_recv()

        def x_copy(m, side, sign, i, hops):
            w = x_part(m, mod(px - sign * hops, NX), side if i != 1 else 1 - side)
            return remote(w, w, uxs.at[m - 1, side, i], uxr.at[m - 1, side, i], at_x(sign))

        def along_x(m):
            for i in range(2):
                for side, sign in sides:
                    go(x_copy(m, side, sign, i, 0))

        def forward_x(m):
            for side, sign in sides:
                x_copy(m, side, sign, 0, 1).wait_recv()
                go(x_copy(m, side, sign, 2, 1))

        def from_x(m):
            for side, sign in sides:
                x_copy(m, side, sign, 1, 1).wait_recv()
                x_copy(m, side, sign, 2, 2).wait_recv()

        for k in (1, 3, 2):
            w = wg.at[ds(py * (NX * GROWS) + mod(px - k, NX) * GROWS, GROWS), ALL]
            remote(w, w, gxs.at[k - 1], gxr.at[k - 1], at_x(k)).wait_recv()
        chain(0)
        from_y(1)
        along_x(1)
        chain(1)
        from_y(2)
        along_x(2)
        forward_x(1)
        chain(2)
        forward_x(2)
        chain(3)
        from_x(1)
        chain(4)
        from_x(2)
        for c in started:
            c.wait_send()

    @pl.when(core == 0)
    def _():
        for c in wloads:
            c.wait()

    def gather_rows(first, count, pad, perm, dst):
        @pl.loop(0, 4)
        def _(n):
            cols = ds(n * 256, 256)
            rows = recv[first : first + count, :, cols].reshape(count * BLK, 256)
            dst[:, cols] = dot(perm[...], rows).astype(BF16)

        xl, xr = dst[0:pad, :], dst[pad : 2 * pad, :]
        dl, dr = dst[2 * pad : 3 * pad, :], dst[3 * pad :, :]
        a = dot(xl, wg[:HALF, :]) + dot(xr, wg[HALF:, :])
        b = dot(xl, wu[:HALF, :]) + dot(xr, wu[HALF:, :])
        dh = dot_nt(dl, wd[:, :HALF]) + dot_nt(dr, wd[:, HALF:])
        s = 1.0 / (1.0 + jnp.exp(-a))
        act = a * s
        hf = act * b
        da = (dh * b * s * (1.0 + a * (1.0 - s))).astype(BF16)
        db = (dh * act).astype(BF16)
        return hf, da, db

    def results(first, count, pad, perm_t, src, hf, da, db):
        h = hf.astype(BF16)
        for n in range(4):
            q, c0 = n // 2, QCOL * (n % 2)
            cols = slice(n * QCOL, (n + 1) * QCOL)
            src[q * pad : (q + 1) * pad, c0 : c0 + QCOL] = dot(h, wd[:, cols]).astype(BF16)
            grad = dot_nt(da, wg[cols, :]) + dot_nt(db, wu[cols, :])
            src[(2 + q) * pad : (3 + q) * pad, c0 : c0 + QCOL] = grad.astype(BF16)

        @pl.loop(0, 4)
        def _(n):
            cols = ds(n * 256, 256)
            rsend[first : first + count, :, cols] = (
                dot(perm_t[...], src[:, cols]).astype(BF16).reshape(count, BLK, 256)
            )

    for c in loads[2:]:
        c.wait()
    backs = []
    for e in exp_far:
        there(*e, whence(e)).wait_recv()
    hf_far, da_far, db_far = gather_rows(0, FAR, FPAD, pf, xf)

    @pl.when(core == 0)
    def _():
        results(0, FAR, FPAD, pft, yf, hf_far, da_far, db_far)

    self_out.wait()
    for e in exp_near:
        there(*e, whence(e)).wait_recv()

    @pl.when(core == 0)
    def _():
        for e in exp_far:
            back(*e, whence(e)).start()

    hf, da, db = gather_rows(FAR, NEAR, NPAD, pn, xn)

    htf = jnp.transpose(hf_far).astype(BF16)
    htn = jnp.transpose(hf).astype(BF16)
    for j in range(NX):
        q, c0 = 2 + j // 2, QCOL * (j % 2)
        piece = dot(htf, xf[q * FPAD : (q + 1) * FPAD, c0 : c0 + QCOL])
        piece = piece + dot(htn, xn[q * NPAD : (q + 1) * NPAD, c0 : c0 + QCOL])
        dw[j] = piece
        for g in range(2):
            dwb[g, j] = piece[:, g * GCOL : (g + 1) * GCOL].astype(BF16)
    right, left, across = mod(px + 1, NX), mod(px - 1, NX), mod(px + 2, NX)
    lo, hi = slice(0, MID), slice(MID, FFW)
    dx_copies = []
    for g in range(2):
        for i, (to, rr, side) in enumerate(
            ((across, lo, 1), (across, hi, -1), (right, hi, 1), (left, lo, -1))
        ):
            dst = (opp if i < 2 else pure).at[g, i % 2]
            c = remote(dwb.at[g, to, rr], dst, dxs.at[g, i], dxr.at[g, i], at_x(side))
            c.start()
            dx_copies.append(c)

    @pl.when(core == 1)
    def _():
        results(0, FAR, FPAD, pft, yf, hf_far, da_far, db_far)
        for e in exp_far:
            back(*e, whence(e)).start()

    backs += [back(*e, whence(e)) for e in exp_far]
    results(FAR, NEAR, NPAD, pnt, yn, hf, da, db)
    for e in exp_near[0:3:2]:
        c = back(*e, whence(e))
        c.start()
        backs.append(c)
    self_back = pltpu.make_async_copy(rsend.at[mine_k], rrecv.at[mine_q], loc_sem.at[10])
    self_back.start()

    halves = [slice(g * GCOL, (g + 1) * GCOL) for g in range(2)]
    merged = []
    for g in range(2):
        for i, (to, rr, side) in enumerate(((right, lo, 1), (left, hi, -1))):
            dx_copies[4 * g + i].wait_recv()
            msend[g, i] = (dw[to, rr, halves[g]] + opp[g, i].astype(F32)).astype(BF16)
            c = remote(msend.at[g, i], mrecv.at[g, i], dxs.at[g, 4 + i], dxr.at[g, 4 + i],
                       at_x(side))
            c.start()
            merged.append(c)
    dy_copies = []
    for g in range(2):
        for c in dx_copies[4 * g + 2 : 4 * g + 4] + merged[2 * g : 2 * g + 2]:
            c.wait_recv()
        for i in range(NY):
            top = i < NY // 2
            rr = slice(i * DROWS, (i + 1) * DROWS)
            r0 = i * DROWS - (0 if top else MID)
            rm = slice(r0, r0 + DROWS)
            m, p = (0, 1) if top else (1, 0)
            got = mrecv[g, m, rm, :].astype(F32) + pure[g, p, rm, :].astype(F32)
            got = dw[px, rr, halves[g]] + got
            ysum[i, :, halves[g]] = got
            yb[g, i] = got.astype(BF16)
        for k in (4, 3, 5, 2, 6, 1, 7):
            c = remote(yb.at[g, mod(py + k, NY)], yrecv.at[g, k - 1], dys.at[g, k - 1],
                       dyr.at[g, k - 1], at_y(k))
            c.start()
            dy_copies.append(c)
    sums, dz = [], []
    for g in range(2):
        for c in dy_copies[g * (NY - 1) : (g + 1) * (NY - 1)]:
            c.wait_recv()
        got = ysum[py, :, halves[g]]
        for k in range(NY - 1):
            got = got + yrecv[g, k].astype(F32)
        sums.append(got)
        zsend[g] = got.astype(BF16)
        c = remote(zsend.at[g], zrecv.at[g], dzs.at[g], dzr.at[g], at_z(8, other))
        dz.append(c)

        @pl.when(core == 1)
        def _():
            c.start()

    for e in exp_near[1:4:2] + exp_near[4:]:
        c = back(*e, whence(e))
        c.start()
        backs.append(c)

    def taking(b, first, count):
        rows = slice(first * BLK, (first + count) * BLK)
        return jnp.where(wantc[b : b + 1, rows] == tgt_c, 1.0, 0.0).astype(BF16)

    takes = [taking(b, 0, FAR) for b in range(4)]
    for e in src_far:
        back(*e, towards(e)).wait_recv()
    for n in range(4):
        cols = slice(n * 256, (n + 1) * 256)
        src = rrecv[0:FAR, :, cols].reshape(FROWS, 256)
        for b in range(4):
            oacc[b, :, cols] = dot(takes[b], src)

    def fin_copies():
        fins = [remote(fsend.at[2 * px + 1], frecv.at[px], fs.at[0, 1], fr.at[px],
                       dev(py, px, 1, pz))]
        for k in range(1, NX):
            to = mod(px + k, NX)
            for c in range(2):
                fins.append(
                    remote(fsend.at[2 * to + c], frecv.at[px], fs.at[k, c], fr.at[px],
                           dev(py, to, c, pz))
                )
        return fins

    mine = pltpu.make_async_copy(fsend.at[2 * px], frecv.at[px], loc_sem.at[11])

    @pl.when(core == 0)
    def _():
        total = []
        for g in range(2):
            dz[g].wait_recv()
            total.append(sums[g] + zrecv[g].astype(F32))
        total = jnp.concatenate(total, axis=1)
        for i in range(2 * NX):
            fsend[i, 0:6, :] = total[i * 6 : (i + 1) * 6, :]
            fsend[i, 6:8, :] = jnp.zeros((2, QCOL), F32)
        mine.start()
        for c in fin_copies():
            c.start()

    takes = [taking(b, FAR, NEAR) for b in range(4)]
    self_back.wait()
    for e in src_near:
        back(*e, towards(e)).wait_recv()
    gsum = jnp.zeros((TOK, 1), F32)
    for n in range(4):
        cols = slice(n * 256, (n + 1) * 256)
        src = rrecv[FAR:, :, cols].reshape(NROWS, 256)
        for q in range(2):
            full = slice(q * HALF + n * 256, q * HALF + (n + 1) * 256)
            o = oacc[q, :, cols] + dot(takes[q], src)
            out_ref[:, full] = (gw_c * o).astype(BF16)
            gsum = gsum + jnp.sum(cot[:, full].astype(F32) * o, axis=1, keepdims=True)
            tgrad_ref[:, full] = (oacc[2 + q, :, cols] + dot(takes[2 + q], src)).astype(BF16)
    ggrad_ref[...] = jnp.sum(jnp.where(eye, gsum, 0.0), axis=0, keepdims=True)
    gone = [
        pltpu.make_async_copy(s, d, res_sem.at[i])
        for i, (s, d) in enumerate(
            ((out_ref, out_hbm), (tgrad_ref, tgrad_hbm), (ggrad_ref, ggrad_hbm),
             (dgrad_ref, dgrad_hbm))
        )
    ]
    for c in gone[:3]:
        c.start()

    @pl.when(core == 0)
    def _():
        mine.wait()
        for k in range(1, NX):
            src = mod(px + k, NX)
            remote(fsend.at[0], frecv.at[src], fs.at[k, 0], fr.at[src],
                   dev(py, src, 0, pz)).wait_recv()
        for c in fin_copies():
            c.wait_send()

    @pl.when(core == 1)
    def _():
        for src in range(NX):
            remote(fsend.at[0], frecv.at[src], fs.at[0, 0], fr.at[src],
                   dev(py, src, 0, pz)).wait_recv()
        for c in dz:
            c.wait_send()

    for j in range(NX):
        for i in range(6):
            dgrad_ref[i, :, j * QCOL : (j + 1) * QCOL] = frecv[j, i : i + 1, :]
    gone[3].start()

    for c in outs + backs + dx_copies + merged + dy_copies:
        c.wait_send()
    for c in gone:
        c.wait()


def hand_over(*refs):
    src, dst, held, (into, out) = refs[:4], refs[4:8], refs[8:12], refs[12:]
    parts = []
    for i in range(2):
        for r in range(2):
            parts.append((i, pl.ds(r * (TOK // 2), TOK // 2)))
    parts += [(2, ALL), (3, ALL)]
    ins = [
        pltpu.make_async_copy(src[i].at[r], held[i].at[r], into.at[n])
        for n, (i, r) in enumerate(parts)
    ]
    outs = [
        pltpu.make_async_copy(held[i].at[r], dst[i].at[r], out.at[n])
        for n, (i, r) in enumerate(parts)
    ]
    for c in ins:
        c.start()
    for c, d in zip(ins, outs):
        c.wait()
        d.start()
    for d in outs:
        d.wait()


def gathering(count, pad):
    perm = np.zeros((4 * pad, count * BLK), np.float32)
    for r in range(count * BLK):
        k, w = divmod(r, BLK)
        half, w = divmod(w, 2 * CAP)
        kind, s = divmod(w, CAP)
        perm[(kind * 2 + half) * pad + k * CAP + s, r] = 1.0
    return jnp.asarray(perm, BF16), jnp.asarray(perm.T, BF16)


def wanted():
    want = np.full((8, NZ * BLK), -1, np.int32)
    for r in range(NZ * BLK):
        k, w = divmod(r, BLK)
        half, w = divmod(w, 2 * CAP)
        kind, s = divmod(w, CAP)
        want[kind * 2 + half, r] = k * CAP + s
    return jnp.asarray(want)


def shards(tokens, expert_ids, gate_weights, cotangent, gate_weight, up_weight, down_weight):
    hbm = pl.BlockSpec(memory_space=pl.ANY)
    vmem = pl.BlockSpec(memory_space=pltpu.VMEM)
    dma = pltpu.SemaphoreType.DMA
    mem = pltpu.VMEM
    outs = (
        jax.ShapeDtypeStruct((TOK, WIDTH), BF16),
        jax.ShapeDtypeStruct((TOK, WIDTH), BF16),
        jax.ShapeDtypeStruct((1, TOK), F32),
        jax.ShapeDtypeStruct((FFW // (2 * NX * NY), 1, WIDTH), F32),
    )
    results = pl.pallas_call(
        kernel,
        out_shape=outs,
        in_specs=[hbm, hbm, vmem, vmem] + [hbm] * 7 + [vmem],
        out_specs=(hbm,) * 4,
        scratch_shapes=[
            mem((TOK, WIDTH), BF16), mem((TOK, WIDTH), BF16), mem((4 * TOK, HALF), BF16),
            mem((WIDTH, FFW), BF16), mem((WIDTH, FFW), BF16), mem((FFW, WIDTH), BF16),
            mem((4 * FPAD, FROWS), BF16), mem((FROWS, 4 * FPAD), BF16),
            mem((4 * NPAD, NROWS), BF16), mem((NROWS, 4 * NPAD), BF16),
            mem((NZ, BLK, HALF), BF16), mem((NZ, BLK, HALF), BF16),
            mem((4 * FPAD, HALF), BF16), mem((4 * FPAD, HALF), BF16),
            mem((4 * NPAD, HALF), BF16), mem((4 * NPAD, HALF), BF16),
            mem((NZ, BLK, HALF), BF16), mem((NZ, BLK, HALF), BF16),
            mem((4, TOK, HALF), F32),
            mem((NX, FFW, QCOL), F32), mem((2, NX, FFW, GCOL), BF16),
            mem((2, 2, MID, GCOL), BF16), mem((2, 2, MID, GCOL), BF16),
            mem((2, 2, MID, GCOL), BF16), mem((2, 2, MID, GCOL), BF16),
            mem((NY, DROWS, QCOL), F32), mem((2, NY, DROWS, GCOL), BF16),
            mem((2, NY - 1, DROWS, GCOL), BF16),
            mem((2, DROWS, GCOL), BF16), mem((2, DROWS, GCOL), BF16),
            mem((2 * NX, 8, QCOL), F32), mem((NX, 8, QCOL), F32),
            dma((12,)),
            dma((NZ,)), dma((NZ,)), dma((NZ,)), dma((NZ,)),
            dma((3,)), dma((3,)), dma((3,)), dma((3,)),
            dma((2, 4)), dma((2, 4)), dma((2, NY - 1)), dma((2, NY - 1)),
            dma((2, 2, 3)), dma((2, 2, 3)),
            dma((2, 6)), dma((2, 6)), dma((2, NY - 1)), dma((2, NY - 1)),
            dma((2,)), dma((2,)), dma((NX, 2)), dma((NX,)), pltpu.SemaphoreType.REGULAR,
            *[mem(o.shape, o.dtype) for o in outs], dma((4,)),
        ],
        compiler_params=pltpu.CompilerParams(
            collective_id=0, has_side_effects=True, vmem_limit_bytes=56 * 1024 * 1024
        ),
        cost_estimate=pl.CostEstimate(
            flops=6_000_000_000, bytes_accessed=16_000_000, transcendentals=100_000
        ),
    )(
        tokens, cotangent, expert_ids.reshape(1, TOK), gate_weights.reshape(1, TOK),
        gate_weight[0], up_weight[0], down_weight[0],
        *gathering(FAR, FPAD), *gathering(NEAR, NPAD), wanted(),
    )
    out, tgrad, ggrad, dgrad = pl.pallas_call(
        hand_over,
        out_shape=outs,
        in_specs=[hbm] * 4,
        out_specs=(hbm,) * 4,
        scratch_shapes=[mem(o.shape, o.dtype) for o in outs] + [dma((6,)), dma((6,))],
        cost_estimate=pl.CostEstimate(flops=0, bytes_accessed=2_200_000, transcendentals=0),
    )(*results)
    return out, tgrad, ggrad.reshape(TOK, 1), jnp.transpose(dgrad, (1, 0, 2))


def solution(mesh):
    rows = P(("rep", "ep"), None)
    weight = P("ep", None, None)
    return jax.shard_map(
        shards,
        mesh=mesh,
        in_specs=(rows, rows, rows, rows, weight, weight, weight),
        out_specs=(rows, rows, rows, P("ep", "rep", None)),
        check_vma=False,
    )
```

```python
import jax
import jax.numpy as jnp
import numpy as np
from jax import lax
from jax.experimental import pallas as pl
from jax.experimental.pallas import tpu as pltpu
from jax.sharding import PartitionSpec as P

NX, NY, NZ = 4, 8, 16
TOK, WIDTH, FFW = 128, 2048, 384
CAP = 12
HALF = WIDTH // 2
BLK = 4 * CAP
FAR = 6
NEAR = NZ - FAR
FROWS, NROWS = FAR * BLK, NEAR * BLK
FPAD, NPAD = 80, 128
GROWS = WIDTH // (NX * NY)
DROWS = FFW // NY
QCOL = WIDTH // NX
MID = FFW // 2
GCOL = QCOL // 2
MESH = pl.DeviceIdType.MESH
F32 = jnp.float32
BF16 = jnp.bfloat16
NT = (((1,), (1,)), ((), ()))
ALL = slice(None)


def dot(a, b):
    return jnp.dot(a, b, preferred_element_type=F32)


def dot_nt(a, b):
    return lax.dot_general(a, b, NT, preferred_element_type=F32)


def ds(start, size):
    return pl.ds(pl.multiple_of(start, size), size)


def kernel(
    x_hbm, cot_hbm, ids_row, gw_row, wg_hbm, wu_hbm, wd_hbm, pf_hbm, pft_hbm, pn_hbm, pnt_hbm,
    wantc,
    out_hbm, tgrad_hbm, ggrad_hbm, dgrad_hbm,
    x, cot, z, wg, wu, wd, pf, pft, pn, pnt, send, recv, xf, yf, xn, yn, rsend, rrecv,
    oacc, dw, dwb, opp, pure, msend, mrecv, ysum, yb, yrecv, zsend, zrecv, fsend, frecv,
    loc_sem, s1, r1, s2, r2, wzs, wzr, gxs, gxr, gys, gyr, uys, uyr, uxs, uxr,
    dxs, dxr, dys, dyr, dzs, dzr, fs, fr, go_sem, out_ref, tgrad_ref, ggrad_ref, dgrad_ref,
    res_sem,
):
    rep = lax.axis_index("rep")
    pz = lax.axis_index("ep")
    core = lax.rem(rep, 2)
    px = lax.rem(rep // 2, NX)
    py = rep // (2 * NX)
    other = 1 - core

    def dev(y, x_, c, z_):
        return ((y * NX + x_) * 2 + c, z_)

    def mod(v, n):
        return lax.rem(v + n, n)

    def at_x(k):
        return dev(py, mod(px + k, NX), core, pz)

    def at_y(k):
        return dev(mod(py + k, NY), px, core, pz)

    def at_z(off, c):
        return dev(py, px, c, mod(pz + off, NZ))

    def remote(src, dst, ss, rs, target):
        return pltpu.make_async_remote_copy(
            src_ref=src, dst_ref=dst, send_sem=ss, recv_sem=rs,
            device_id=target, device_id_type=MESH,
        )

    tie, tie_other = 4 - 8 * core, 4 - 8 * other
    barrier = pltpu.get_barrier_semaphore()
    peers = [at_z(8, core), at_z(8, other), at_z(-4, core), at_z(4, core), at_z(tie, other)]
    for k in (4, 3, 5, 2, 6, 1, 7):
        peers.append(at_y(k))
    for o in (-3, 3, -2, 2, -1, 1):
        peers += [at_z(o, core), at_z(o, other)]
    for k in (2, 1, 3):
        peers.append(at_x(k))
        peers.append(dev(py, mod(px + k, NX), other, pz))
    peers.append(at_z(0, other))
    for peer in peers:
        pl.semaphore_signal(barrier, inc=1, device_id=peer, device_id_type=MESH)

    loads = [
        pltpu.make_async_copy(s, d, loc_sem.at[i])
        for i, (s, d) in enumerate(
            ((x_hbm, x), (cot_hbm, cot), (pf_hbm, pf), (pft_hbm, pft), (pn_hbm, pn), (pnt_hbm, pnt))
        )
    ]
    for c in loads:
        c.start()
    weights = (wg, wu, wd)
    wloads = [
        pltpu.make_async_copy(s, d, loc_sem.at[6 + i])
        for i, (s, d) in enumerate(zip((wg_hbm, wu_hbm, wd_hbm), weights))
    ]

    @pl.when(core == 0)
    def _():
        for c in wloads:
            c.start()

    def place_of(ids):
        u = lax.rem(ids - pz + (2 * NZ - 3), NZ)
        u = u + jnp.where((u >= 3) & (u < 8), 3, 0) - jnp.where((u >= 8) & (u < 11), 5, 0)
        return u

    lane = lax.broadcasted_iota(jnp.int32, (TOK, TOK), 1)
    sub = lax.broadcasted_iota(jnp.int32, (TOK, TOK), 0)
    eye = lane == sub
    q_r = place_of(ids_row[...])
    q_c = jnp.sum(jnp.where(eye, q_r, 0), axis=1, keepdims=True)
    gw_c = jnp.sum(jnp.where(eye, gw_row[...], 0.0), axis=1, keepdims=True)
    oh_r = (lax.broadcasted_iota(jnp.int32, (NZ, TOK), 0) == q_r).astype(F32)
    before = dot(oh_r.astype(BF16), (sub < lane).astype(F32).astype(BF16))
    slot_r = jnp.sum(before * oh_r, axis=0, keepdims=True).astype(jnp.int32)
    tgt_r = q_r * CAP + slot_r
    tgt_c = jnp.sum(jnp.where(eye, tgt_r, 0), axis=1, keepdims=True)

    def placing(first, count):
        ex = lax.broadcasted_iota(jnp.int32, (count, BLK, TOK), 0) + first
        row = lax.broadcasted_iota(jnp.int32, (count, BLK, TOK), 1)
        half = jnp.where(row >= 2 * CAP, 1, 0)
        row = row - 2 * CAP * half
        kind = jnp.where(row >= CAP, 1, 0)
        want = ex * CAP + row - CAP * kind
        quarter = jnp.where(want == tgt_r.reshape(1, 1, TOK), kind * 2 + half, -1)
        return jnp.concatenate(
            [
                jnp.where(quarter == b, 1.0, 0.0).reshape(count * BLK, TOK).astype(BF16)
                for b in range(4)
            ],
            axis=1,
        )

    place_far = placing(0, FAR)
    for c in loads[:2]:
        c.wait()
    z[0:TOK, :] = x[:, :HALF]
    z[TOK : 2 * TOK, :] = x[:, HALF:]
    dout = (gw_c * cot[...].astype(F32)).astype(BF16)
    z[2 * TOK : 3 * TOK, :] = dout[:, :HALF]
    z[3 * TOK :, :] = dout[:, HALF:]

    def build(place, first, count):
        @pl.loop(0, 4)
        def _(n):
            cols = ds(n * 256, 256)
            send[first : first + count, :, cols] = (
                dot(place, z[:, cols]).astype(BF16).reshape(count, BLK, 256)
            )

    build(place_far, 0, FAR)
    pl.semaphore_wait(barrier, len(peers))

    own = (
        (ds(py * (NX * GROWS) + px * GROWS, GROWS), ALL),
        (ds(px * (NY * GROWS) + py * GROWS, GROWS), ALL),
        (ds(py * DROWS, DROWS), ds(px * QCOL, QCOL)),
    )
    wz = [
        remote(h.at[i], w.at[i], wzs.at[m], wzr.at[m], at_z(8, core))
        for m, (h, w, i) in enumerate(zip((wg_hbm, wu_hbm, wd_hbm), weights, own))
    ]

    @pl.when(core == 1)
    def _():
        for m in (1, 2, 0):
            wz[m].start()

    def as_source():
        far = [(tie, core, 1, 4 + core), (tie, other, 4, 4 + core)]
        for c in (core, other):
            far += [(3, c, 3 * c, 2 + core), (-3, c, 5 - 3 * c, core)]
        near = []
        for o in (2, -2, 1, -1):
            for c in (core, other):
                near.append((o, c, 13 + o - 5 * c, 10 + 2 * o + core))
        near.append((0, other, 13 - 5 * other, 10 + core))
        return far, near

    def as_expert():
        far = [(tie, core, 1, 4 + core), (tie_other, other, 4, 4 + other)]
        for c in (core, other):
            far += [(3, c, 3 * core, 2 + c), (-3, c, 5 - 3 * core, c)]
        near = []
        for o in (2, -2, 1, -1):
            for c in (core, other):
                near.append((o, c, 13 + o - 5 * core, 10 + 2 * o + c))
        near.append((0, other, 13 - 5 * core, 10 + other))
        return far, near

    def there(off, c, q, k, target):
        return remote(send.at[q], recv.at[k], s1.at[q], r1.at[k], target)

    def back(off, c, q, k, target):
        return remote(rsend.at[k], rrecv.at[q], s2.at[k], r2.at[q], target)

    def towards(e):
        return at_z(e[0], e[1])

    def whence(e):
        return at_z(-e[0], e[1])

    mine_q, mine_k = 13 - 5 * core, 10 + core
    src_far, src_near = as_source()
    exp_far, exp_near = as_expert()

    outs = [there(*e, towards(e)) for e in src_far]
    for c in outs:
        c.start()
    build(placing(FAR, NEAR), FAR, NEAR)

    def y_slice(m, y):
        if m == 0:
            return wg.at[ds(y * (NX * GROWS), NX * GROWS), ALL]
        if m == 1:
            return wu.at[ds(px * (NY * GROWS) + y * GROWS, GROWS), ALL]
        return wd.at[ds(y * DROWS, DROWS), ds(px * QCOL, QCOL)]

    def first_copies(m):
        if m == 0:
            w = wg.at[own[0]]
            return [remote(w, w, gxs.at[k - 1], gxr.at[k - 1], at_x(k)) for k in (2, 1, 3)]
        w = y_slice(m, py)
        return [
            remote(w, w, uys.at[m - 1, k - 1], uyr.at[m - 1, k - 1], at_y(k))
            for k in (4, 3, 5, 2, 6, 1, 7)
        ]

    @pl.when(core == 1)
    def _():
        for m in (1, 2, 0):
            wz[m].wait_recv()
            for c in first_copies(m):
                c.start()
        pl.semaphore_signal(go_sem, inc=1, device_id=at_z(0, other), device_id_type=MESH)

    @pl.when(core == 0)
    def _():
        pl.semaphore_wait(go_sem, 1)

    for e in src_near:
        c = there(*e, towards(e))
        c.start()
        outs.append(c)
    self_out = pltpu.make_async_copy(send.at[mine_q], recv.at[mine_k], loc_sem.at[9])
    self_out.start()

    @pl.when(core == 1)
    def _():
        started = wz + first_copies(0) + first_copies(1) + first_copies(2)

        def go(c):
            c.start()
            started.append(c)

        sides = ((0, 1), (1, -1))

        def chain(step):
            for side, sign in sides:
                w = y_slice(0, mod(py - sign * step, NY))
                if step == 4:
                    w = w.at[half_rows[side]]
                if step > 0:
                    remote(w, w, gys.at[side, step - 1], gyr.at[side, step - 1],
                           at_y(sign)).wait_recv()
                if step == 3:
                    w = w.at[half_rows[side]]
                if step < 4:
                    go(remote(w, w, gys.at[side, step], gyr.at[side, step], at_y(sign)))

        half_rows = [slice(i * (GROWS * NX // 2), (i + 1) * (GROWS * NX // 2)) for i in range(2)]

        def x_part(m, xx, part):
            if m == 1:
                n = NY * GROWS
                return wu.at[ds(xx * n + part * (n // 2), n // 2), ALL]
            return wd.at[part * MID : (part + 1) * MID, ds(xx * QCOL, QCOL)]

        def from_y(m):
            for k in (1, 7, 2, 6, 3, 5, 4):
                w = y_slice(m, mod(py - k, NY))
                remote(w, w, uys.at[m - 1, k - 1], uyr.at[m - 1, k - 1], at_y(k)).wait_recv()

        def x_copy(m, side, sign, i, hops):
            w = x_part(m, mod(px - sign * hops, NX), side if i != 1 else 1 - side)
            return remote(w, w, uxs.at[m - 1, side, i], uxr.at[m - 1, side, i], at_x(sign))

        def along_x(m):
            for i in range(2):
                for side, sign in sides:
                    go(x_copy(m, side, sign, i, 0))

        def forward_x(m):
            for side, sign in sides:
                x_copy(m, side, sign, 0, 1).wait_recv()
                go(x_copy(m, side, sign, 2, 1))

        def from_x(m):
            for side, sign in sides:
                x_copy(m, side, sign, 1, 1).wait_recv()
                x_copy(m, side, sign, 2, 2).wait_recv()

        for k in (1, 3, 2):
            w = wg.at[ds(py * (NX * GROWS) + mod(px - k, NX) * GROWS, GROWS), ALL]
            remote(w, w, gxs.at[k - 1], gxr.at[k - 1], at_x(k)).wait_recv()
        chain(0)
        from_y(1)
        along_x(1)
        chain(1)
        from_y(2)
        along_x(2)
        forward_x(1)
        chain(2)
        forward_x(2)
        chain(3)
        from_x(1)
        chain(4)
        from_x(2)
        for c in started:
            c.wait_send()

    @pl.when(core == 0)
    def _():
        for c in wloads:
            c.wait()

    def gather_rows(first, count, pad, perm, dst):
        @pl.loop(0, 4)
        def _(n):
            cols = ds(n * 256, 256)
            rows = recv[first : first + count, :, cols].reshape(count * BLK, 256)
            dst[:, cols] = dot(perm[...], rows).astype(BF16)

        xl, xr = dst[0:pad, :], dst[pad : 2 * pad, :]
        dl, dr = dst[2 * pad : 3 * pad, :], dst[3 * pad :, :]
        a = dot(xl, wg[:HALF, :]) + dot(xr, wg[HALF:, :])
        b = dot(xl, wu[:HALF, :]) + dot(xr, wu[HALF:, :])
        dh = dot_nt(dl, wd[:, :HALF]) + dot_nt(dr, wd[:, HALF:])
        s = 1.0 / (1.0 + jnp.exp(-a))
        act = a * s
        hf = act * b
        da = (dh * b * s * (1.0 + a * (1.0 - s))).astype(BF16)
        db = (dh * act).astype(BF16)
        return hf, da, db

    def results(first, count, pad, perm_t, src, hf, da, db):
        h = hf.astype(BF16)
        for n in range(4):
            q, c0 = n // 2, QCOL * (n % 2)
            cols = slice(n * QCOL, (n + 1) * QCOL)
            src[q * pad : (q + 1) * pad, c0 : c0 + QCOL] = dot(h, wd[:, cols]).astype(BF16)
            grad = dot_nt(da, wg[cols, :]) + dot_nt(db, wu[cols, :])
            src[(2 + q) * pad : (3 + q) * pad, c0 : c0 + QCOL] = grad.astype(BF16)

        @pl.loop(0, 4)
        def _(n):
            cols = ds(n * 256, 256)
            rsend[first : first + count, :, cols] = (
                dot(perm_t[...], src[:, cols]).astype(BF16).reshape(count, BLK, 256)
            )

    for c in loads[2:]:
        c.wait()
    backs = []
    for e in exp_far:
        there(*e, whence(e)).wait_recv()
    hf_far, da_far, db_far = gather_rows(0, FAR, FPAD, pf, xf)

    @pl.when(core == 0)
    def _():
        results(0, FAR, FPAD, pft, yf, hf_far, da_far, db_far)

    self_out.wait()
    for e in exp_near:
        there(*e, whence(e)).wait_recv()

    @pl.when(core == 0)
    def _():
        for e in exp_far:
            back(*e, whence(e)).start()

    hf, da, db = gather_rows(FAR, NEAR, NPAD, pn, xn)

    htf = jnp.transpose(hf_far).astype(BF16)
    htn = jnp.transpose(hf).astype(BF16)
    for j in range(NX):
        q, c0 = 2 + j // 2, QCOL * (j % 2)
        piece = dot(htf, xf[q * FPAD : (q + 1) * FPAD, c0 : c0 + QCOL])
        piece = piece + dot(htn, xn[q * NPAD : (q + 1) * NPAD, c0 : c0 + QCOL])
        dw[j] = piece
        for g in range(2):
            dwb[g, j] = piece[:, g * GCOL : (g + 1) * GCOL].astype(BF16)
    right, left, across = mod(px + 1, NX), mod(px - 1, NX), mod(px + 2, NX)
    lo, hi = slice(0, MID), slice(MID, FFW)
    dx_copies = []
    for g in range(2):
        for i, (to, rr, side) in enumerate(
            ((across, lo, 1), (across, hi, -1), (right, hi, 1), (left, lo, -1))
        ):
            dst = (opp if i < 2 else pure).at[g, i % 2]
            c = remote(dwb.at[g, to, rr], dst, dxs.at[g, i], dxr.at[g, i], at_x(side))
            c.start()
            dx_copies.append(c)

    @pl.when(core == 1)
    def _():
        results(0, FAR, FPAD, pft, yf, hf_far, da_far, db_far)
        for e in exp_far:
            back(*e, whence(e)).start()

    backs += [back(*e, whence(e)) for e in exp_far]
    results(FAR, NEAR, NPAD, pnt, yn, hf, da, db)
    self_back = pltpu.make_async_copy(rsend.at[mine_k], rrecv.at[mine_q], loc_sem.at[10])
    self_back.start()

    halves = [slice(g * GCOL, (g + 1) * GCOL) for g in range(2)]
    merged = []
    for g in range(2):
        for i, (to, rr, side) in enumerate(((right, lo, 1), (left, hi, -1))):
            dx_copies[4 * g + i].wait_recv()
            msend[g, i] = (dw[to, rr, halves[g]] + opp[g, i].astype(F32)).astype(BF16)
            c = remote(msend.at[g, i], mrecv.at[g, i], dxs.at[g, 4 + i], dxr.at[g, 4 + i],
                       at_x(side))
            c.start()
            merged.append(c)
    dy_copies = []
    for g in range(2):
        for c in dx_copies[4 * g + 2 : 4 * g + 4] + merged[2 * g : 2 * g + 2]:
            c.wait_recv()
        for i in range(NY):
            top = i < NY // 2
            rr = slice(i * DROWS, (i + 1) * DROWS)
            r0 = i * DROWS - (0 if top else MID)
            rm = slice(r0, r0 + DROWS)
            m, p = (0, 1) if top else (1, 0)
            got = mrecv[g, m, rm, :].astype(F32) + pure[g, p, rm, :].astype(F32)
            got = dw[px, rr, halves[g]] + got
            ysum[i, :, halves[g]] = got
            yb[g, i] = got.astype(BF16)
        for k in (4, 3, 5, 2, 6, 1, 7):
            c = remote(yb.at[g, mod(py + k, NY)], yrecv.at[g, k - 1], dys.at[g, k - 1],
                       dyr.at[g, k - 1], at_y(k))
            c.start()
            dy_copies.append(c)
    for e in exp_near[0:3:2]:
        c = back(*e, whence(e))
        c.start()
        backs.append(c)
    sums, dz = [], []
    for g in range(2):
        for c in dy_copies[g * (NY - 1) : (g + 1) * (NY - 1)]:
            c.wait_recv()
        got = ysum[py, :, halves[g]]
        for k in range(NY - 1):
            got = got + yrecv[g, k].astype(F32)
        sums.append(got)
        zsend[g] = got.astype(BF16)
        c = remote(zsend.at[g], zrecv.at[g], dzs.at[g], dzr.at[g], at_z(8, other))
        dz.append(c)

        @pl.when(core == 1)
        def _():
            c.start()

    for e in exp_near[1:4:2] + exp_near[4:]:
        c = back(*e, whence(e))
        c.start()
        backs.append(c)

    def taking(b, first, count):
        rows = slice(first * BLK, (first + count) * BLK)
        return jnp.where(wantc[b : b + 1, rows] == tgt_c, 1.0, 0.0).astype(BF16)

    takes = [taking(b, 0, FAR) for b in range(4)]
    for e in src_far:
        back(*e, towards(e)).wait_recv()
    for n in range(4):
        cols = slice(n * 256, (n + 1) * 256)
        src = rrecv[0:FAR, :, cols].reshape(FROWS, 256)
        for b in range(4):
            oacc[b, :, cols] = dot(takes[b], src)

    def fin_copies():
        fins = [remote(fsend.at[2 * px + 1], frecv.at[px], fs.at[0, 1], fr.at[px],
                       dev(py, px, 1, pz))]
        for k in range(1, NX):
            to = mod(px + k, NX)
            for c in range(2):
                fins.append(
                    remote(fsend.at[2 * to + c], frecv.at[px], fs.at[k, c], fr.at[px],
                           dev(py, to, c, pz))
                )
        return fins

    mine = pltpu.make_async_copy(fsend.at[2 * px], frecv.at[px], loc_sem.at[11])

    @pl.when(core == 0)
    def _():
        total = []
        for g in range(2):
            dz[g].wait_recv()
            total.append(sums[g] + zrecv[g].astype(F32))
        total = jnp.concatenate(total, axis=1)
        for i in range(2 * NX):
            fsend[i, 0:6, :] = total[i * 6 : (i + 1) * 6, :]
            fsend[i, 6:8, :] = jnp.zeros((2, QCOL), F32)
        mine.start()
        for c in fin_copies():
            c.start()

    takes = [taking(b, FAR, NEAR) for b in range(4)]
    self_back.wait()
    for e in src_near:
        back(*e, towards(e)).wait_recv()
    gsum = jnp.zeros((TOK, 1), F32)
    for n in range(4):
        cols = slice(n * 256, (n + 1) * 256)
        src = rrecv[FAR:, :, cols].reshape(NROWS, 256)
        for q in range(2):
            full = slice(q * HALF + n * 256, q * HALF + (n + 1) * 256)
            o = oacc[q, :, cols] + dot(takes[q], src)
            out_ref[:, full] = (gw_c * o).astype(BF16)
            gsum = gsum + jnp.sum(cot[:, full].astype(F32) * o, axis=1, keepdims=True)
            tgrad_ref[:, full] = (oacc[2 + q, :, cols] + dot(takes[2 + q], src)).astype(BF16)
    ggrad_ref[...] = jnp.sum(jnp.where(eye, gsum, 0.0), axis=0, keepdims=True)
    gone = [
        pltpu.make_async_copy(s, d, res_sem.at[i])
        for i, (s, d) in enumerate(
            ((out_ref, out_hbm), (tgrad_ref, tgrad_hbm), (ggrad_ref, ggrad_hbm),
             (dgrad_ref, dgrad_hbm))
        )
    ]
    for c in gone[:3]:
        c.start()

    @pl.when(core == 0)
    def _():
        mine.wait()
        for k in range(1, NX):
            src = mod(px + k, NX)
            remote(fsend.at[0], frecv.at[src], fs.at[k, 0], fr.at[src],
                   dev(py, src, 0, pz)).wait_recv()
        for c in fin_copies():
            c.wait_send()

    @pl.when(core == 1)
    def _():
        for src in range(NX):
            remote(fsend.at[0], frecv.at[src], fs.at[0, 0], fr.at[src],
                   dev(py, src, 0, pz)).wait_recv()
        for c in dz:
            c.wait_send()

    for j in range(NX):
        for i in range(6):
            dgrad_ref[i, :, j * QCOL : (j + 1) * QCOL] = frecv[j, i : i + 1, :]
    gone[3].start()

    for c in outs + backs + dx_copies + merged + dy_copies:
        c.wait_send()
    for c in gone:
        c.wait()


def hand_over(*refs):
    src, dst, held, (into, out) = refs[:4], refs[4:8], refs[8:12], refs[12:]
    parts = []
    for i in range(2):
        for r in range(2):
            parts.append((i, pl.ds(r * (TOK // 2), TOK // 2)))
    parts += [(2, ALL), (3, ALL)]
    ins = [
        pltpu.make_async_copy(src[i].at[r], held[i].at[r], into.at[n])
        for n, (i, r) in enumerate(parts)
    ]
    outs = [
        pltpu.make_async_copy(held[i].at[r], dst[i].at[r], out.at[n])
        for n, (i, r) in enumerate(parts)
    ]
    for c in ins:
        c.start()
    for c, d in zip(ins, outs):
        c.wait()
        d.start()
    for d in outs:
        d.wait()


def gathering(count, pad):
    perm = np.zeros((4 * pad, count * BLK), np.float32)
    for r in range(count * BLK):
        k, w = divmod(r, BLK)
        half, w = divmod(w, 2 * CAP)
        kind, s = divmod(w, CAP)
        perm[(kind * 2 + half) * pad + k * CAP + s, r] = 1.0
    return jnp.asarray(perm, BF16), jnp.asarray(perm.T, BF16)


def wanted():
    want = np.full((8, NZ * BLK), -1, np.int32)
    for r in range(NZ * BLK):
        k, w = divmod(r, BLK)
        half, w = divmod(w, 2 * CAP)
        kind, s = divmod(w, CAP)
        want[kind * 2 + half, r] = k * CAP + s
    return jnp.asarray(want)


def shards(tokens, expert_ids, gate_weights, cotangent, gate_weight, up_weight, down_weight):
    hbm = pl.BlockSpec(memory_space=pl.ANY)
    vmem = pl.BlockSpec(memory_space=pltpu.VMEM)
    dma = pltpu.SemaphoreType.DMA
    mem = pltpu.VMEM
    outs = (
        jax.ShapeDtypeStruct((TOK, WIDTH), BF16),
        jax.ShapeDtypeStruct((TOK, WIDTH), BF16),
        jax.ShapeDtypeStruct((1, TOK), F32),
        jax.ShapeDtypeStruct((FFW // (2 * NX * NY), 1, WIDTH), F32),
    )
    results = pl.pallas_call(
        kernel,
        out_shape=outs,
        in_specs=[hbm, hbm, vmem, vmem] + [hbm] * 7 + [vmem],
        out_specs=(hbm,) * 4,
        scratch_shapes=[
            mem((TOK, WIDTH), BF16), mem((TOK, WIDTH), BF16), mem((4 * TOK, HALF), BF16),
            mem((WIDTH, FFW), BF16), mem((WIDTH, FFW), BF16), mem((FFW, WIDTH), BF16),
            mem((4 * FPAD, FROWS), BF16), mem((FROWS, 4 * FPAD), BF16),
            mem((4 * NPAD, NROWS), BF16), mem((NROWS, 4 * NPAD), BF16),
            mem((NZ, BLK, HALF), BF16), mem((NZ, BLK, HALF), BF16),
            mem((4 * FPAD, HALF), BF16), mem((4 * FPAD, HALF), BF16),
            mem((4 * NPAD, HALF), BF16), mem((4 * NPAD, HALF), BF16),
            mem((NZ, BLK, HALF), BF16), mem((NZ, BLK, HALF), BF16),
            mem((4, TOK, HALF), F32),
            mem((NX, FFW, QCOL), F32), mem((2, NX, FFW, GCOL), BF16),
            mem((2, 2, MID, GCOL), BF16), mem((2, 2, MID, GCOL), BF16),
            mem((2, 2, MID, GCOL), BF16), mem((2, 2, MID, GCOL), BF16),
            mem((NY, DROWS, QCOL), F32), mem((2, NY, DROWS, GCOL), BF16),
            mem((2, NY - 1, DROWS, GCOL), BF16),
            mem((2, DROWS, GCOL), BF16), mem((2, DROWS, GCOL), BF16),
            mem((2 * NX, 8, QCOL), F32), mem((NX, 8, QCOL), F32),
            dma((12,)),
            dma((NZ,)), dma((NZ,)), dma((NZ,)), dma((NZ,)),
            dma((3,)), dma((3,)), dma((3,)), dma((3,)),
            dma((2, 4)), dma((2, 4)), dma((2, NY - 1)), dma((2, NY - 1)),
            dma((2, 2, 3)), dma((2, 2, 3)),
            dma((2, 6)), dma((2, 6)), dma((2, NY - 1)), dma((2, NY - 1)),
            dma((2,)), dma((2,)), dma((NX, 2)), dma((NX,)), pltpu.SemaphoreType.REGULAR,
            *[mem(o.shape, o.dtype) for o in outs], dma((4,)),
        ],
        compiler_params=pltpu.CompilerParams(
            collective_id=0, has_side_effects=True, vmem_limit_bytes=56 * 1024 * 1024
        ),
        cost_estimate=pl.CostEstimate(
            flops=6_000_000_000, bytes_accessed=16_000_000, transcendentals=100_000
        ),
    )(
        tokens, cotangent, expert_ids.reshape(1, TOK), gate_weights.reshape(1, TOK),
        gate_weight[0], up_weight[0], down_weight[0],
        *gathering(FAR, FPAD), *gathering(NEAR, NPAD), wanted(),
    )
    out, tgrad, ggrad, dgrad = pl.pallas_call(
        hand_over,
        out_shape=outs,
        in_specs=[hbm] * 4,
        out_specs=(hbm,) * 4,
        scratch_shapes=[mem(o.shape, o.dtype) for o in outs] + [dma((6,)), dma((6,))],
        cost_estimate=pl.CostEstimate(flops=0, bytes_accessed=2_200_000, transcendentals=0),
    )(*results)
    return out, tgrad, ggrad.reshape(TOK, 1), jnp.transpose(dgrad, (1, 0, 2))


def solution(mesh):
    rows = P(("rep", "ep"), None)
    weight = P("ep", None, None)
    return jax.shard_map(
        shards,
        mesh=mesh,
        in_specs=(rows, rows, rows, rows, weight, weight, weight),
        out_specs=(rows, rows, rows, P("ep", "rep", None)),
        check_vma=False,
    )
```
